32 devices in a mesh: groups: 2 (over x), seq: 16 (over z, y, core).
Axes of the slice: x: 2, y: 2, z: 4, core: 2. Of those that a mesh axis runs over, the one named last changes fastest.
Arguments:
- tokens: bfloat16 [32768, 1024], P(('groups', 'seq')), parts along dimension 0, may hold values from -6 to 6
- doc_start: int32 [32768], P(('groups', 'seq')), parts along dimension 0, may hold values from 0 to 1
- level_index: int32 [32768], P(('groups', 'seq')), parts along dimension 0, may hold values from 0 to 63
- level_table: float32 [64, 18], replicated, may hold values from 0.0004 to 4.1, as said below
- conv_weight: float32 [4, 1024], replicated, may hold values from -3 to 3
- query_weight: bfloat16 [1024, 1024], replicated, may hold values from -0.1875 to 0.1875
- key_weight: bfloat16 [1024, 1024], replicated, may hold values from -0.1875 to 0.1875
- value_weight: bfloat16 [1024, 1024], replicated, may hold values from -0.1875 to 0.1875
- norm_gain: float32 [1024], replicated, may hold values from 0.5 to 1.5
Outputs:
- mixed: bfloat16 [32768, 1024], P(('groups', 'seq')), parts along dimension 0
The draws below stay inside these ranges and needn't reach their ends.
There are 2 independent parts, one for each index of `groups`. The reference program is written for one: setup_inputs(seed, part) draws one part's arguments, and reference() takes and returns one part's arrays. A program takes and returns all parts, laid end to end along the dimension named above; an argument that names none is the same for every part. Nothing has to cross between parts.
Inputs may be any that keep to these rules, and one draw needn't show every extreme that they name: `level_table`: positive entries.
All inputs are finite; a program needn't handle non-finite values.
Results may differ from the reference program's by a relative error of at most 0.007.
Values may be sent and summed in bfloat16 or wider, within the bound.
A program may use at most 128 MiB of HBM per device.

```python
import jax
import jax.numpy as jnp
from jax import lax

D = 1024
HEADS = 8
HEAD_DIM = 128
CONV = 4
LEVELS = 18
TABLE = 64
TOK_DEV = 1024
TOKENS = 16384
N_SEQ = 16


def draw_doc_start(key, part):
    draw_rate = max(TOK_DEV // 2, 1)
    picked = jax.random.randint(jax.random.fold_in(key, 11), (TOKENS,), 0, draw_rate)
    position = jnp.arange(TOKENS, dtype=jnp.int32)
    inside = (position >= TOKENS // 8) & (position < TOKENS * 3 // 8)
    return ((picked == 0) & inside).astype(jnp.int32)


def draw_level_table(key, part):
    level_ids = jnp.arange(LEVELS, dtype=jnp.float32)
    spread = jax.random.uniform(jax.random.fold_in(key, 5), (TABLE, LEVELS), jnp.float32, -0.7, 0.7)
    return jnp.exp(spread) * jnp.exp2(-0.5 * level_ids)[None, :]


def plant(values, rng, low, top_value):
    place = [jax.random.randint(jax.random.fold_in(rng, axis), (), 0, length) for axis, length in enumerate(values.shape)]
    longest = values.shape.index(max(values.shape))
    beside = place[:longest] + [(place[longest] + 1) % values.shape[longest]] + place[longest + 1:]
    return values.at[tuple(place)].set(low).at[tuple(beside)].set(top_value)


def shard_levels(rng, extent, cuts, smallest, largest):
    factor_of = 1.0
    for dim, parts in cuts:
        draws = jax.random.uniform(jax.random.fold_in(jax.random.fold_in(rng, 6), dim), (parts,), jnp.float32, smallest / len(cuts), largest / len(cuts))
        factor_of = factor_of * jnp.repeat(jnp.exp(draws), extent[dim] // parts).reshape((-1,) + (1,) * (len(extent) - 1 - dim))
    return factor_of


def bell_draw(stream_key, extent, deviation, reach, split=(), held_as=jnp.bfloat16):
    gain = shard_levels(stream_key, extent, split, -0.22, 0.18) if split else 1.0
    values = jax.random.normal(stream_key, extent, jnp.float32) * deviation * gain
    return jnp.minimum(jnp.maximum(values, -reach), reach).astype(held_as)


def setup_inputs(seed: int = 0, part: int = 0) -> dict:
    key_of = jax.random.split(jax.random.key(seed), 10)
    part_splits = jax.random.split(jax.random.fold_in(key_of[9], part), 10)
    return {
        "tokens": bell_draw(part_splits[0], (TOKENS, D), 1.0, 6.0, ((0, 16),)),
        "doc_start": draw_doc_start(jax.random.fold_in(jax.random.fold_in(key_of[9], part), 71), part),
        "level_index": plant(jax.random.randint(part_splits[2], (TOKENS,), 0, TABLE), jax.random.fold_in(part_splits[2], 1), 0, TABLE - 1).astype(jnp.int32),
        "level_table": draw_level_table(jax.random.fold_in(key_of[9], 71), part),
        "conv_weight": bell_draw(key_of[4], (CONV, D), 0.5, 3.0, (), jnp.float32),
        "query_weight": bell_draw(key_of[5], (D, D), D ** -0.5, 0.1875),
        "key_weight": bell_draw(key_of[6], (D, D), D ** -0.5, 0.1875),
        "value_weight": bell_draw(key_of[7], (D, D), D ** -0.5, 0.1875),
        "norm_gain": jnp.clip(1.0 + 0.1 * jax.random.normal(key_of[8], (D,), jnp.float32), 0.5, 1.5),
    }


highest = lax.Precision.HIGHEST
epsilon = 1e-05

def bit_count(values, bit_width):
    counted = jnp.zeros_like(values)
    for bit_index in range(bit_width):
        counted = counted + (values >= 1 << bit_index).astype(jnp.int32)
    return counted

def reference(tokens, doc_start, level_index, level_table, conv_weight, query_weight, key_weight, value_weight, norm_gain):
    tap_count = conv_weight.shape[0]
    doc_id = jnp.cumsum(doc_start).astype(jnp.int32)
    padded = jnp.concatenate([jnp.zeros((tap_count - 1, D), tokens.dtype), tokens], 0)
    doc_pad = jnp.concatenate([jnp.full((tap_count - 1,), -1, jnp.int32), doc_id], 0)
    conv_sum = jnp.zeros((TOKENS, D), jnp.float32)
    for tap_index in range(tap_count):
        low_row = tap_count - 1 - tap_index
        shifted = padded[low_row:low_row + TOKENS].astype(jnp.float32)
        same_doc = (doc_pad[low_row:low_row + TOKENS] == doc_id).astype(jnp.float32)
        conv_sum = conv_sum + conv_weight[tap_index][None, :] * shifted * same_doc[:, None]
    conv_out = conv_sum.astype(jnp.bfloat16)
    queries = jnp.dot(conv_out, query_weight, preferred_element_type=jnp.float32).astype(jnp.bfloat16)
    key_rows = jnp.dot(conv_out, key_weight, preferred_element_type=jnp.float32).astype(jnp.bfloat16)
    values = jnp.dot(conv_out, value_weight, preferred_element_type=jnp.float32).astype(jnp.bfloat16)
    level_weight = level_table[level_index]
    block_count = N_SEQ
    local_bits = TOK_DEV.bit_length() - 1
    chain_bits = N_SEQ.bit_length() - 1
    query_blocks = queries.reshape(block_count, TOK_DEV, HEADS, HEAD_DIM)
    key_blocks = key_rows.reshape(block_count, TOK_DEV, HEADS, HEAD_DIM)
    value_blocks = values.reshape(block_count, TOK_DEV, HEADS, HEAD_DIM)
    doc_blocks = doc_id.reshape(block_count, TOK_DEV)
    weight_blocks = level_weight.reshape(block_count, TOK_DEV, LEVELS)
    last_doc = doc_blocks[:, TOK_DEV - 1]
    tail_mask = (doc_blocks == last_doc[:, None]).astype(jnp.float32)
    key_tail = key_blocks.astype(jnp.float32) * tail_mask[:, :, None, None]
    states = jnp.einsum('bnhd,bnhe->bhde', key_tail, value_blocks.astype(jnp.float32), precision=highest)
    positions = jnp.arange(TOK_DEV, dtype=jnp.int32)
    level_local = bit_count(jnp.bitwise_xor(positions[:, None], positions[None, :]), local_bits)
    causal = positions[:, None] >= positions[None, :]
    blocks = jnp.arange(block_count, dtype=jnp.int32)
    gain_heads = norm_gain.reshape(HEADS, HEAD_DIM)

    def one_block(inputs):
        block_index, query_here, key_here, value_here, doc_here, weight_here = inputs
        same_doc = (doc_here[:, None] == doc_here[None, :]) & causal
        weight = jnp.zeros((TOK_DEV, TOK_DEV), jnp.float32)
        for level_id in range(local_bits + 1):
            weight = weight + jnp.where(level_local == level_id, weight_here[:, level_id:level_id + 1], 0.0)
        weight = jnp.where(same_doc, weight, 0.0)
        scores = jnp.einsum('thd,shd->hts', query_here.astype(jnp.float32), key_here.astype(jnp.float32))
        weighted = (scores * weight[None]).astype(jnp.bfloat16)
        near_sum = jnp.einsum('hts,shd->thd', weighted.astype(jnp.float32), value_here.astype(jnp.float32))
        first_doc = doc_here[0]
        earlier = (last_doc == first_doc) & (blocks < block_index)
        token_gate = (doc_here == first_doc).astype(jnp.float32)
        level_far = bit_count(jnp.bitwise_xor(blocks, block_index), chain_bits) - 1
        query_wide = query_here.astype(jnp.float32)
        combined = near_sum
        for bit_index in range(chain_bits):
            selector = (earlier & (level_far == bit_index)).astype(jnp.float32)
            level_state = jnp.einsum('b,bhde->hde', selector, states, precision=highest)
            product = jnp.einsum('thd,hde->the', query_wide, level_state, precision=highest)
            scale_now = weight_here[:, local_bits + 1 + bit_index] * token_gate
            combined = combined + scale_now[:, None, None] * product
        inv_norm = lax.rsqrt(lax.optimization_barrier(jnp.mean(combined * combined, axis=-1, keepdims=True)) + epsilon)
        return (combined * inv_norm * gain_heads[None]).reshape(TOK_DEV, D).astype(jnp.bfloat16)
    results = lax.map(one_block, (blocks, query_blocks, key_blocks, value_blocks, doc_blocks, weight_blocks))
    return results.reshape(TOKENS, D)
```

```python
import functools

import jax
import jax.numpy as jnp
from jax import lax
from jax.experimental import pallas as pl
from jax.experimental.pallas import tpu as pltpu
from jax.sharding import PartitionSpec as P

HEADS = 8
HEAD_DIM = 128
LANES = 128
EDGE = 16

highest = lax.Precision.HIGHEST
epsilon = 1e-05
f32 = jnp.float32
bf16 = jnp.bfloat16


def dot(a, b, contract=((1,), (0,)), precision=None):
    return lax.dot_general(a, b, (contract, ((), ())), precision=precision, preferred_element_type=f32)


def layer(
    count,
    ds_ref, li_ref, table_ref, taps_ref, gain_ref, tok_ref, wq_hbm, wk_hbm, wv_hbm,
    out_ref,
    wq, wk, wv, turn, docs, dext, tail, lam, lamfar, weight, ext, conv, q, k, v, near,
    state, agg, flag_agg, flag_before, coef, send, recv, rim, halo,
    w_sem, send_sem, recv_sem, fwd_send, fwd_recv, rim_sem,
):
    rows, width = tok_ref.shape
    tiles = rows // LANES
    taps = taps_ref.shape[0]
    bits = count.bit_length() - 1
    local_bits = rows.bit_length() - 1
    tile_bits = LANES.bit_length() - 1
    half_heads = HEADS // 2
    half = half_heads * HEAD_DIM
    me = lax.axis_index("seq")
    core = lax.rem(me, 2)
    sibling = me + 1 - 2 * core

    def side(bit):
        return lax.rem(me // (1 << bit), 2)

    def partner(bit):
        return me + (1 - 2 * side(bit)) * (1 << bit)

    ahead, behind = lax.rem(me + 1, count), lax.rem(me + count - 1, count)
    barrier = pltpu.get_barrier_semaphore()
    greeted = [ahead, behind] + [partner(bit) for bit in range(bits)]
    for other in greeted:
        pl.semaphore_signal(barrier, inc=1, device_id={"seq": other}, device_id_type=pl.DeviceIdType.MESH)

    loads = [
        pltpu.make_async_copy(src, dst, w_sem.at[i])
        for i, (src, dst) in enumerate(((wk_hbm, wk), (wv_hbm, wv), (wq_hbm, wq)))
    ]
    for load in loads:
        load.start()

    def remote(src, dst, s_sem, r_sem, to):
        return pltpu.make_async_remote_copy(
            src_ref=src, dst_ref=dst, send_sem=s_sem, recv_sem=r_sem,
            device_id={"seq": to}, device_id_type=pl.DeviceIdType.MESH,
        )

    sub = lax.broadcasted_iota(jnp.int32, (LANES, LANES), 0)
    lane = lax.broadcasted_iota(jnp.int32, (LANES, LANES), 1)
    upper = (sub <= lane).astype(f32).astype(bf16)
    counted = dot(ds_ref[...].astype(f32).astype(bf16), upper)
    running = jnp.zeros((1, 1), f32)
    turn[...] = jnp.zeros_like(turn)
    for i in range(tiles):
        turn[i : i + 1, :] = counted[i : i + 1, :] + running
        docs[i : i + 1, :] = counted[i : i + 1, :] + running
        running = running + counted[i : i + 1, LANES - 1 : LANES]
    turn[tiles : 2 * tiles, :] = li_ref[...].astype(f32)
    turned = jnp.transpose(turn[...])
    last_doc = running
    dext[0:8, :] = jnp.zeros((8, LANES), f32)
    for i in range(tiles):
        column = jnp.broadcast_to(turned[:, i : i + 1], (LANES, LANES))
        dext[8 + i * LANES : 8 + (i + 1) * LANES, :] = column
        tail[i * LANES : (i + 1) * LANES, :] = (column == last_doc).astype(f32).astype(bf16)
    own_open = jnp.broadcast_to((last_doc == 0.0).astype(f32), (8, LANES))
    flag_agg[...] = own_open
    flag_before[...] = jnp.ones((8, LANES), f32)

    for j in range(width // LANES):
        cols = slice(j * LANES, (j + 1) * LANES)
        rim[:, cols] = tok_ref[rows - EDGE : rows, cols] * tail[rows - EDGE : rows, :]
    pl.semaphore_wait(barrier, len(greeted))
    rim_copy = remote(rim, halo, rim_sem.at[0], rim_sem.at[1], ahead)

    @pl.when(me < count - 1)
    def _():
        rim_copy.start()

    chunk = 64

    def conv_chunk(first):
        ext[pl.ds(8 + first, chunk), :] = tok_ref[pl.ds(first, chunk), :].astype(f32)
        window = pl.ds(first, chunk + 8)
        docs_here = dext[window, :]
        same = [(pltpu.roll(docs_here, t, 0) == docs_here).astype(f32)[8:] for t in range(1, taps)]
        for j in range(width // LANES):
            cols = slice(j * LANES, (j + 1) * LANES)
            values = ext[window, cols]
            total = taps_ref[0:1, cols] * values[8:]
            for t in range(1, taps):
                total = total + taps_ref[t : t + 1, cols] * pltpu.roll(values, t, 0)[8:] * same[t - 1]
            conv[pl.ds(first, chunk), cols] = total.astype(bf16)

    ext[8 : 8 + chunk, :] = tok_ref[0:chunk, :].astype(f32)

    @pl.loop(1, rows // chunk)
    def _(i):
        conv_chunk(pl.multiple_of(i * chunk, chunk))

    @pl.when(me > 0)
    def _():
        rim_copy.wait_recv()

    @pl.when(me == 0)
    def _():
        halo[...] = jnp.zeros_like(halo)

    ext[0:8, :] = halo[...].astype(f32)[EDGE - 8 : EDGE, :]
    conv_chunk(0)

    def project(w, out, i):
        cols = pl.ds(pl.multiple_of(i * 2 * HEAD_DIM, 2 * HEAD_DIM), 2 * HEAD_DIM)
        made = dot(conv[...], w[:, cols]).astype(bf16)
        out[2 * i] = made[:, :HEAD_DIM]
        out[2 * i + 1] = made[:, HEAD_DIM:]

    loads[0].wait()
    loads[1].wait()

    @pl.loop(0, HEADS // 2)
    def _(i):
        project(wk, k, i)
        project(wv, v, i)
        for s in range(2):
            h = 2 * i + s
            made = dot(k[h] * tail[...], v[h], ((0,), (0,)))
            at = pl.ds(pl.multiple_of(lax.rem(h, half_heads) * HEAD_DIM, HEAD_DIM), HEAD_DIM)
            state[h // half_heads, at, :] = made
            send[0, h // half_heads, at, :] = made.astype(bf16)

    flag_rows = jnp.concatenate([own_open, own_open], 0).astype(bf16)
    for s in range(2):
        send[0, s, half : half + EDGE, :] = flag_rows
    first = remote(send.at[0], recv.at[0], send_sem.at[0], recv_sem.at[0], sibling)
    first.start()

    def step(bit):
        return remote(send.at[bit, core], recv.at[bit, core], send_sem.at[bit], recv_sem.at[bit], partner(bit))

    def forward(bit):
        return remote(recv.at[bit, core], recv.at[bit, core], fwd_send.at[bit], fwd_recv.at[bit], sibling)

    def note_flags(bit):
        other = recv[bit, core, half : half + EDGE, :].astype(f32)[0:8]
        right = side(bit).astype(f32)
        before = flag_before[...]
        coef[bit] = right * before
        flag_before[...] = before * ((1.0 - right) + right * other)
        return other, right

    def absorb(bit):
        other, right = note_flags(bit)
        mine = flag_agg[...]
        of_agg = (right + (1.0 - right) * other)[0:1]
        of_other = ((1.0 - right) + right * mine)[0:1]
        source = state.at[core] if bit == 0 else agg
        total = of_agg * source[...] + of_other * recv[bit, core, 0:half, :].astype(f32)
        agg[...] = total
        send[bit + 1, core, 0:half, :] = total.astype(bf16)
        joined = mine * other
        flag_agg[...] = joined
        send[bit + 1, core, half : half + EDGE, :] = jnp.concatenate([joined, joined], 0).astype(bf16)
        step(bit + 1).start()

    loads[2].wait()

    @pl.loop(0, HEADS // 2)
    def _(i):
        project(wq, q, i)

    first.wait_recv()
    absorb(0)

    table = table_ref[...]
    pick = lax.broadcasted_iota(jnp.int32, (LANES, table.shape[0]), 1).astype(f32)
    apart = jnp.bitwise_xor(sub, lane)
    for i in range(tiles):
        chosen = (turned[:, tiles + i : tiles + i + 1] == pick).astype(f32)
        lam[i * LANES : (i + 1) * LANES, :] = dot(chosen, table, precision=highest)
    for i in range(tiles):
        at = slice(i * LANES, (i + 1) * LANES)
        here = lam[at, :]
        doc = dext[8 + i * LANES : 8 + (i + 1) * LANES, :]

        def spread(level):
            return jnp.broadcast_to(here[:, level : level + 1], (LANES, LANES))

        tile = spread(0)
        for level in range(1, tile_bits + 1):
            tile = jnp.where(apart >= 1 << (level - 1), spread(level), tile)
        weight[at, at] = jnp.where((doc == docs[i : i + 1, :]) & (sub >= lane), tile, 0.0)
        if i % 2 == 0:
            weight[at, (i + 1) * LANES : (i + 2) * LANES] = jnp.zeros((LANES, LANES), f32)
        wide = {}
        for j in range(i):
            level = tile_bits + (i ^ j).bit_length()
            if level not in wide:
                wide[level] = spread(level)
            weight[at, j * LANES : (j + 1) * LANES] = jnp.where(doc == docs[j : j + 1, :], wide[level], 0.0)
        for bit in range(bits):
            lamfar[bit, at, :] = jnp.where(doc == 0.0, spread(local_bits + 1 + bit), 0.0)

    block = min(2 * LANES, rows)
    events = {(bit * HEADS) // max(bits - 1, 1) - 1: bit for bit in range(1, bits - 1)}

    @pl.loop(0, HEADS)
    def _(h):
        for r in range(rows // block):
            at = slice(r * block, (r + 1) * block)
            upto = (r + 1) * block
            scores = dot(q[h, at, :], k[h, 0:upto, :], ((1,), (1,)))
            weighted = (scores * weight[at, 0:upto]).astype(bf16)
            near[h, at, :] = dot(weighted, v[h, 0:upto, :])
        for after, bit in events.items():

            @pl.when(h == after)
            def _():
                step(bit).wait_recv()
                forward(bit).start()
                absorb(bit)

    def far_state(bit, h):
        at = pl.ds(pl.multiple_of(lax.rem(h, half_heads) * HEAD_DIM, HEAD_DIM), HEAD_DIM)
        found = recv[bit, h // half_heads, at, :].astype(f32)
        return (found * coef[bit][0:1]).astype(bf16)

    for bit in range(1, bits - 1):
        forward(bit).wait_recv()

    early = list(range(bits - 1))

    @pl.loop(0, HEADS)
    def _(h):
        for r in range(rows // block):
            at = slice(r * block, (r + 1) * block)
            total = near[h, at, :]
            for a in range(0, len(early), 2):
                pair = early[a : a + 2]
                found = [far_state(bit, h) for bit in pair]
                made = dot(q[h, at, :], jnp.concatenate(found, 1) if len(found) > 1 else found[0])
                for n, bit in enumerate(pair):
                    total = total + lamfar[bit, at, :] * made[:, n * HEAD_DIM : (n + 1) * HEAD_DIM]
            near[h, at, :] = total

    last = bits - 1
    step(last).wait_recv()
    forward(last).start()
    note_flags(last)
    forward(last).wait_recv()

    @pl.loop(0, HEADS)
    def _(h):
        cols = pl.ds(pl.multiple_of(h * HEAD_DIM, HEAD_DIM), HEAD_DIM)
        gain = gain_ref[:, cols]
        found = far_state(last, h)
        for r in range(rows // block):
            at = slice(r * block, (r + 1) * block)
            total = near[h, at, :] + lamfar[last, at, :] * dot(q[h, at, :], found)
            scale = lax.rsqrt(jnp.mean(total * total, axis=-1, keepdims=True) + epsilon)
            out_ref[at, cols] = (total * scale * gain).astype(bf16)

    @pl.when(me < count - 1)
    def _():
        rim_copy.wait_send()

    first.wait_send()
    for bit in range(1, bits):
        step(bit).wait_send()
        forward(bit).wait_send()


def shards(
    tokens, doc_start, level_index, level_table, conv_weight, query_weight, key_weight, value_weight, norm_gain
):
    rows, width = tokens.shape
    count = lax.axis_size("seq")
    bits = count.bit_length() - 1
    half = HEADS // 2 * HEAD_DIM
    heads = (HEADS, rows, HEAD_DIM)
    vmem = pl.BlockSpec(memory_space=pltpu.VMEM)
    hbm = pl.BlockSpec(memory_space=pl.ANY)
    dma = pltpu.SemaphoreType.DMA
    return pl.pallas_call(
        functools.partial(layer, count),
        out_shape=jax.ShapeDtypeStruct((rows, width), bf16),
        in_specs=[vmem] * 6 + [hbm] * 3,
        out_specs=vmem,
        scratch_shapes=[
            pltpu.VMEM((width, width), bf16),
            pltpu.VMEM((width, width), bf16),
            pltpu.VMEM((width, width), bf16),
            pltpu.VMEM((LANES, LANES), f32),
            pltpu.VMEM((rows // LANES, LANES), f32),
            pltpu.VMEM((rows + 8, LANES), f32),
            pltpu.VMEM((rows, LANES), bf16),
            pltpu.VMEM((rows, level_table.shape[1]), f32),
            pltpu.VMEM((bits, rows, LANES), f32),
            pltpu.VMEM((rows, rows), f32),
            pltpu.VMEM((rows + 8, width), f32),
            pltpu.VMEM((rows, width), bf16),
            pltpu.VMEM(heads, bf16),
            pltpu.VMEM(heads, bf16),
            pltpu.VMEM(heads, bf16),
            pltpu.VMEM(heads, f32),
            pltpu.VMEM((2, half, HEAD_DIM), f32),
            pltpu.VMEM((half, HEAD_DIM), f32),
            pltpu.VMEM((8, LANES), f32),
            pltpu.VMEM((8, LANES), f32),
            pltpu.VMEM((bits, 8, LANES), f32),
            pltpu.VMEM((bits, 2, half + EDGE, HEAD_DIM), bf16),
            pltpu.VMEM((bits, 2, half + EDGE, HEAD_DIM), bf16),
            pltpu.VMEM((EDGE, width), bf16),
            pltpu.VMEM((EDGE, width), bf16),
            dma((3,)),
            dma((bits,)),
            dma((bits,)),
            dma((bits,)),
            dma((bits,)),
            dma((2,)),
        ],
        compiler_params=pltpu.CompilerParams(
            collective_id=0, has_side_effects=True, vmem_limit_bytes=56 * 1024 * 1024
        ),
    )(
        doc_start.reshape(rows // LANES, LANES),
        level_index.reshape(rows // LANES, LANES),
        level_table,
        conv_weight,
        norm_gain.reshape(1, width),
        tokens,
        query_weight,
        key_weight,
        value_weight,
    )


def solution(mesh):
    split = P(("groups", "seq"))
    rows = P(("groups", "seq"), None)
    in_specs = (rows, split, split, P(), P(), P(), P(), P(), P())
    return jax.shard_map(shards, mesh=mesh, in_specs=in_specs, out_specs=rows, check_vma=False)
```

```python
import functools

import jax
import jax.numpy as jnp
from jax import lax
from jax.experimental import pallas as pl
from jax.experimental.pallas import tpu as pltpu
from jax.sharding import PartitionSpec as P

HEADS = 8
HEAD_DIM = 128
LANES = 128
EDGE = 16

highest = lax.Precision.HIGHEST
epsilon = 1e-05
f32 = jnp.float32
bf16 = jnp.bfloat16


def dot(a, b, contract=((1,), (0,)), precision=None):
    return lax.dot_general(a, b, (contract, ((), ())), precision=precision, preferred_element_type=f32)


def layer(
    count,
    ds_ref, li_ref, table_ref, taps_ref, tok_hbm, wq_hbm, wk_hbm, wv_hbm,
    out_hbm,
    tok_ref, out_ref,
    wq, wk, wv, turn, docs, dext, tail, lam, lamfar, weight, ext, conv, q, k, v, near,
    state, agg, flag_agg, flag_before, coef, send, recv, rim, halo,
    w_sem, out_sem, send_sem, recv_sem, fwd_send, fwd_recv, rim_sem,
):
    rows, width = tok_ref.shape
    tiles = rows // LANES
    taps = taps_ref.shape[0]
    bits = count.bit_length() - 1
    local_bits = rows.bit_length() - 1
    tile_bits = LANES.bit_length() - 1
    half_heads = HEADS // 2
    part_heads = half_heads // 2
    part_rows = part_heads * HEAD_DIM
    me = lax.axis_index("seq")
    core = lax.rem(me, 2)
    sibling = me + 1 - 2 * core

    def side(bit):
        return lax.rem(me // (1 << bit), 2)

    def partner(bit):
        return me + (1 - 2 * side(bit)) * (1 << bit)

    ahead, behind = lax.rem(me + 1, count), lax.rem(me + count - 1, count)
    barrier = pltpu.get_barrier_semaphore()
    greeted = [ahead, behind] + [partner(bit) for bit in range(bits)]
    for other in greeted:
        pl.semaphore_signal(barrier, inc=1, device_id={"seq": other}, device_id_type=pl.DeviceIdType.MESH)

    loads = [
        pltpu.make_async_copy(src, dst, w_sem.at[i])
        for i, (src, dst) in enumerate(((tok_hbm, tok_ref), (wk_hbm, wk), (wv_hbm, wv), (wq_hbm, wq)))
    ]
    for load in loads:
        load.start()

    def remote(src, dst, s_sem, r_sem, to):
        return pltpu.make_async_remote_copy(
            src_ref=src, dst_ref=dst, send_sem=s_sem, recv_sem=r_sem,
            device_id={"seq": to}, device_id_type=pl.DeviceIdType.MESH,
        )

    sub = lax.broadcasted_iota(jnp.int32, (LANES, LANES), 0)
    lane = lax.broadcasted_iota(jnp.int32, (LANES, LANES), 1)
    upper = (sub <= lane).astype(f32).astype(bf16)
    counted = dot(ds_ref[...].astype(f32).astype(bf16), upper)
    running = jnp.zeros((1, 1), f32)
    turn[...] = jnp.zeros_like(turn)
    for i in range(tiles):
        turn[i : i + 1, :] = counted[i : i + 1, :] + running
        docs[i : i + 1, :] = counted[i : i + 1, :] + running
        running = running + counted[i : i + 1, LANES - 1 : LANES]
    turn[tiles : 2 * tiles, :] = li_ref[...].astype(f32)
    turned = jnp.transpose(turn[...])
    last_doc = running
    dext[0:8, :] = jnp.zeros((8, LANES), f32)
    for i in range(tiles):
        column = jnp.broadcast_to(turned[:, i : i + 1], (LANES, LANES))
        dext[8 + i * LANES : 8 + (i + 1) * LANES, :] = column
        tail[i * LANES : (i + 1) * LANES, :] = (column == last_doc).astype(f32).astype(bf16)
    own_open = jnp.broadcast_to((last_doc == 0.0).astype(f32), (8, LANES))
    for part in range(2):
        flag_agg[part] = own_open
        flag_before[part] = jnp.ones((8, LANES), f32)

    loads[0].wait()

    for j in range(width // LANES):
        cols = slice(j * LANES, (j + 1) * LANES)
        rim[:, cols] = tok_ref[rows - EDGE : rows, cols] * tail[rows - EDGE : rows, :]
    pl.semaphore_wait(barrier, len(greeted))
    rim_copy = remote(rim, halo, rim_sem.at[0], rim_sem.at[1], ahead)

    @pl.when(me < count - 1)
    def _():
        rim_copy.start()

    chunk = 64

    def conv_chunk(first):
        ext[pl.ds(8 + first, chunk), :] = tok_ref[pl.ds(first, chunk), :].astype(f32)
        window = pl.ds(first, chunk + 8)
        docs_here = dext[window, :]
        same = [(pltpu.roll(docs_here, t, 0) == docs_here).astype(f32)[8:] for t in range(1, taps)]
        for j in range(width // LANES):
            cols = slice(j * LANES, (j + 1) * LANES)
            values = ext[window, cols]
            total = taps_ref[0:1, cols] * values[8:]
            for t in range(1, taps):
                total = total + taps_ref[t : t + 1, cols] * pltpu.roll(values, t, 0)[8:] * same[t - 1]
            conv[pl.ds(first, chunk), cols] = total.astype(bf16)

    ext[8 : 8 + chunk, :] = tok_ref[0:chunk, :].astype(f32)

    @pl.loop(1, rows // chunk)
    def _(i):
        conv_chunk(pl.multiple_of(i * chunk, chunk))

    @pl.when(me > 0)
    def _():
        rim_copy.wait_recv()

    @pl.when(me == 0)
    def _():
        halo[...] = jnp.zeros_like(halo)

    ext[0:8, :] = halo[...].astype(f32)[EDGE - 8 : EDGE, :]
    conv_chunk(0)

    def project(w, out, i):
        cols = pl.ds(pl.multiple_of(i * 2 * HEAD_DIM, 2 * HEAD_DIM), 2 * HEAD_DIM)
        made = dot(conv[...], w[:, cols]).astype(bf16)
        out[2 * i] = made[:, :HEAD_DIM]
        out[2 * i + 1] = made[:, HEAD_DIM:]

    flag_rows = jnp.concatenate([own_open, own_open], 0).astype(bf16)
    for part in range(2):
        for s in range(2):
            send[0, part, s, part_rows : part_rows + EDGE, :] = flag_rows

    def first(part):
        return remote(send.at[0, part], recv.at[0, part], send_sem.at[0, part], recv_sem.at[0, part], sibling)

    loads[1].wait()
    loads[2].wait()

    @pl.loop(0, HEADS // 2)
    def _(n):
        part, side_of = n // 2, lax.rem(n, 2)
        i = 2 * side_of + part
        project(wk, k, i)
        project(wv, v, i)
        for s in range(2):
            h = 2 * i + s
            made = dot(k[h] * tail[...], v[h], ((0,), (0,)))
            at = slice(s * HEAD_DIM, (s + 1) * HEAD_DIM)
            state[part, side_of, at, :] = made
            send[0, part, side_of, at, :] = made.astype(bf16)
        for done in range(2):

            @pl.when(n == 2 * done + 1)
            def _():
                first(done).start()

    def step(bit, part):
        return remote(
            send.at[bit, part, core], recv.at[bit, part, core],
            send_sem.at[bit, part], recv_sem.at[bit, part], partner(bit),
        )

    def forward(bit, part):
        return remote(
            recv.at[bit, part, core], recv.at[bit, part, core],
            fwd_send.at[bit, part], fwd_recv.at[bit, part], sibling,
        )

    def note_flags(bit, part):
        other = recv[bit, part, core, part_rows : part_rows + EDGE, :].astype(f32)[0:8]
        right = side(bit).astype(f32)
        before = flag_before[part]
        coef[bit, part] = right * before
        flag_before[part] = before * ((1.0 - right) + right * other)
        return other, right

    def absorb(bit, part):
        other, right = note_flags(bit, part)
        mine = flag_agg[part]
        of_agg = (right + (1.0 - right) * other)[0:1]
        of_other = ((1.0 - right) + right * mine)[0:1]
        source = state[part, core] if bit == 0 else agg[part]
        total = of_agg * source + of_other * recv[bit, part, core, 0:part_rows, :].astype(f32)
        agg[part] = total
        send[bit + 1, part, core, 0:part_rows, :] = total.astype(bf16)
        joined = mine * other
        flag_agg[part] = joined
        send[bit + 1, part, core, part_rows : part_rows + EDGE, :] = jnp.concatenate([joined, joined], 0).astype(bf16)
        step(bit + 1, part).start()

    def arrive(bit, part):
        step(bit, part).wait_recv()
        forward(bit, part).start()
        if bit < bits - 1:
            absorb(bit, part)
        else:
            note_flags(bit, part)

    last = bits - 1
    steps = [(bit, part) for bit in range(1, last) for part in range(2)]
    events = {0: steps[2:3], HEADS - 1: []}
    for n, event in enumerate(steps[3:]):
        after = min(2 + n, HEADS - 1)
        events[after] = events.get(after, []) + [event]
    events[HEADS - 1] = events[HEADS - 1] + [(last, 0)]

    first(0).wait_recv()
    absorb(0, 0)

    loads[3].wait()

    @pl.loop(0, HEADS // 2)
    def _(i):
        project(wq, q, i)

    first(1).wait_recv()
    absorb(0, 1)
    for event in steps[0:1]:
        arrive(*event)

    table = table_ref[...]
    pick = lax.broadcasted_iota(jnp.int32, (LANES, table.shape[1]), 1).astype(f32)
    apart = jnp.bitwise_xor(sub, lane)
    for i in range(tiles):
        chosen = (turned[:, tiles + i : tiles + i + 1] == pick).astype(f32)
        lam[i * LANES : (i + 1) * LANES, :] = dot(chosen, table, ((1,), (1,)), highest)
    for i in range(tiles):
        at = slice(i * LANES, (i + 1) * LANES)
        here = lam[at, :]
        doc = dext[8 + i * LANES : 8 + (i + 1) * LANES, :]

        def spread(level):
            return jnp.broadcast_to(here[:, level : level + 1], (LANES, LANES))

        tile = spread(0)
        for level in range(1, tile_bits + 1):
            tile = jnp.where(apart >= 1 << (level - 1), spread(level), tile)
        weight[at, at] = jnp.where((doc == docs[i : i + 1, :]) & (sub >= lane), tile, 0.0)
        if i % 2 == 0:
            weight[at, (i + 1) * LANES : (i + 2) * LANES] = jnp.zeros((LANES, LANES), f32)
        wide = {}
        for j in range(i):
            level = tile_bits + (i ^ j).bit_length()
            if level not in wide:
                wide[level] = spread(level)
            weight[at, j * LANES : (j + 1) * LANES] = jnp.where(doc == docs[j : j + 1, :], wide[level], 0.0)
        for bit in range(bits):
            lamfar[bit, at, :] = jnp.where(doc == 0.0, spread(local_bits + 1 + bit), 0.0)

    for event in steps[1:2]:
        arrive(*event)

    block = min(2 * LANES, rows)

    @pl.loop(0, HEADS)
    def _(h):
        for r in range(rows // block):
            at = slice(r * block, (r + 1) * block)
            upto = (r + 1) * block
            scores = dot(q[h, at, :], k[h, 0:upto, :], ((1,), (1,)))
            weighted = (scores * weight[at, 0:upto]).astype(bf16)
            near[h, at, :] = dot(weighted, v[h, 0:upto, :])
        for after, arriving in events.items():

            @pl.when(h == after)
            def _():
                for event in arriving:
                    arrive(*event)

    def far_state(bit, h):
        part = lax.rem(h, half_heads) // part_heads
        at = pl.ds(pl.multiple_of(lax.rem(h, part_heads) * HEAD_DIM, HEAD_DIM), HEAD_DIM)
        found = recv[bit, part, h // half_heads, at, :].astype(f32)
        return (found * coef[bit, 0][0:1]).astype(bf16)

    for bit in range(1, last):
        for part in range(2):
            forward(bit, part).wait_recv()

    early = list(range(bits - 1))

    @pl.loop(0, HEADS)
    def _(h):
        for r in range(rows // block):
            at = slice(r * block, (r + 1) * block)
            total = near[h, at, :]
            for a in range(0, len(early), 2):
                pair = early[a : a + 2]
                found = [far_state(bit, h) for bit in pair]
                made = dot(q[h, at, :], jnp.concatenate(found, 1) if len(found) > 1 else found[0])
                for n, bit in enumerate(pair):
                    total = total + lamfar[bit, at, :] * made[:, n * HEAD_DIM : (n + 1) * HEAD_DIM]
            near[h, at, :] = total

    arrive(last, 1)

    @pl.loop(0, HEADS)
    def _(n):
        @pl.when(n == half_heads)
        def _():
            for part in range(2):
                forward(last, part).wait_recv()

        h = lax.rem(n + core * half_heads, HEADS)
        cols = pl.ds(pl.multiple_of(h * HEAD_DIM, HEAD_DIM), HEAD_DIM)
        found = far_state(last, h)
        for r in range(rows // block):
            at = slice(r * block, (r + 1) * block)
            total = near[h, at, :] + lamfar[last, at, :] * dot(q[h, at, :], found)
            scale = lax.rsqrt(jnp.mean(total * total, axis=-1, keepdims=True) + epsilon)
            out_ref[at, cols] = (total * scale).astype(bf16)
        pltpu.make_async_copy(out_ref.at[:, cols], out_hbm.at[:, cols], out_sem.at[h]).start()

    for h in range(HEADS):
        cols = pl.ds(h * HEAD_DIM, HEAD_DIM)
        pltpu.make_async_copy(out_ref.at[:, cols], out_hbm.at[:, cols], out_sem.at[h]).wait()

    @pl.when(me < count - 1)
    def _():
        rim_copy.wait_send()

    for part in range(2):
        first(part).wait_send()
        for bit in range(1, bits):
            step(bit, part).wait_send()
            forward(bit, part).wait_send()


def shards(
    tokens, doc_start, level_index, level_table, conv_weight, query_weight, key_weight, value_weight, norm_gain
):
    rows, width = tokens.shape
    count = lax.axis_size("seq")
    bits = count.bit_length() - 1
    part_rows = HEADS // 4 * HEAD_DIM
    heads = (HEADS, rows, HEAD_DIM)
    vmem = pl.BlockSpec(memory_space=pltpu.VMEM)
    hbm = pl.BlockSpec(memory_space=pl.ANY)
    dma = pltpu.SemaphoreType.DMA
    made = pl.pallas_call(
        functools.partial(layer, count),
        out_shape=jax.ShapeDtypeStruct((rows, width), bf16),
        in_specs=[vmem] * 4 + [hbm] * 4,
        out_specs=hbm,
        scratch_shapes=[
            pltpu.VMEM((rows, width), bf16),
            pltpu.VMEM((rows, width), bf16),
            pltpu.VMEM((width, width), bf16),
            pltpu.VMEM((width, width), bf16),
            pltpu.VMEM((width, width), bf16),
            pltpu.VMEM((LANES, LANES), f32),
            pltpu.VMEM((rows // LANES, LANES), f32),
            pltpu.VMEM((rows + 8, LANES), f32),
            pltpu.VMEM((rows, LANES), bf16),
            pltpu.VMEM((rows, level_table.shape[1]), f32),
            pltpu.VMEM((bits, rows, LANES), f32),
            pltpu.VMEM((rows, rows), f32),
            pltpu.VMEM((rows + 8, width), f32),
            pltpu.VMEM((rows, width), bf16),
            pltpu.VMEM(heads, bf16),
            pltpu.VMEM(heads, bf16),
            pltpu.VMEM(heads, bf16),
            pltpu.VMEM(heads, f32),
            pltpu.VMEM((2, 2, part_rows, HEAD_DIM), f32),
            pltpu.VMEM((2, part_rows, HEAD_DIM), f32),
            pltpu.VMEM((2, 8, LANES), f32),
            pltpu.VMEM((2, 8, LANES), f32),
            pltpu.VMEM((bits, 2, 8, LANES), f32),
            pltpu.VMEM((bits, 2, 2, part_rows + EDGE, HEAD_DIM), bf16),
            pltpu.VMEM((bits, 2, 2, part_rows + EDGE, HEAD_DIM), bf16),
            pltpu.VMEM((EDGE, width), bf16),
            pltpu.VMEM((EDGE, width), bf16),
            dma((4,)),
            dma((HEADS,)),
            dma((bits, 2)),
            dma((bits, 2)),
            dma((bits, 2)),
            dma((bits, 2)),
            dma((2,)),
        ],
        compiler_params=pltpu.CompilerParams(
            collective_id=0, has_side_effects=True, vmem_limit_bytes=56 * 1024 * 1024
        ),
    )(
        doc_start.reshape(rows // LANES, LANES),
        level_index.reshape(rows // LANES, LANES),
        level_table.T,
        conv_weight,
        tokens,
        query_weight,
        key_weight,
        value_weight,
    )
    return (made.astype(f32) * norm_gain[None, :]).astype(bf16)


def solution(mesh):
    split = P(("groups", "seq"))
    rows = P(("groups", "seq"), None)
    in_specs = (rows, split, split, P(), P(), P(), P(), P(), P())
    return jax.shard_map(shards, mesh=mesh, in_specs=in_specs, out_specs=rows, check_vma=False)
```

```python
import functools

import jax
import jax.numpy as jnp
from jax import lax
from jax.experimental import pallas as pl
from jax.experimental.pallas import tpu as pltpu
from jax.sharding import PartitionSpec as P

HEADS = 8
HEAD_DIM = 128
LANES = 128
PIECES = 4
EDGE = 16

highest = lax.Precision.HIGHEST
epsilon = 1e-05
f32 = jnp.float32
bf16 = jnp.bfloat16


def dot(a, b, contract=((1,), (0,)), precision=None):
    return lax.dot_general(a, b, (contract, ((), ())), precision=precision, preferred_element_type=f32)


def inner_slots(inner):
    groups = [(g, j) for j in range(inner) for g in range(0, 1 << inner, 2 << j)]
    return {group: n for n, group in enumerate(groups)}


def layer(
    count,
    ds_ref, li_ref, table_ref, taps_ref, gain_ref, tok_hbm, wq_hbm, wk_hbm, wv_hbm,
    out_hbm,
    tok_ref, out_ref,
    wq, wk, wv, turn, docs, dext, tail, lam, lamfar, lamloc, local, weight, ext, conv, q, k, v, near,
    state, agg, flag_agg, flag_before, coef, send, recv, rim, halo,
    w_sem, out_sem, send_sem, recv_sem, fwd_send, fwd_recv, rim_sem,
):
    rows, width = tok_ref.shape
    tiles = rows // LANES
    taps = taps_ref.shape[0]
    bits = count.bit_length() - 1
    local_bits = rows.bit_length() - 1
    tile_bits = LANES.bit_length() - 1
    block = min(2 * LANES, rows)
    blocks = rows // block
    block_bits = block.bit_length() - 1
    block_tiles = block // LANES
    inner = local_bits - block_bits
    slots = inner_slots(inner)
    half_heads = HEADS // 2
    part_heads = half_heads // 2
    part_rows = part_heads * HEAD_DIM
    me = lax.axis_index("seq")
    core = lax.rem(me, 2)
    sibling = me + 1 - 2 * core

    def side(bit):
        return lax.rem(me // (1 << bit), 2)

    def partner(bit):
        return me + (1 - 2 * side(bit)) * (1 << bit)

    ahead, behind = lax.rem(me + 1, count), lax.rem(me + count - 1, count)
    barrier = pltpu.get_barrier_semaphore()
    greeted = [ahead, behind] + [partner(bit) for bit in range(bits)]
    for other in greeted:
        pl.semaphore_signal(barrier, inc=1, device_id={"seq": other}, device_id_type=pl.DeviceIdType.MESH)

    loads = [
        pltpu.make_async_copy(src, dst, w_sem.at[i])
        for i, (src, dst) in enumerate(((tok_hbm, tok_ref), (wk_hbm, wk), (wv_hbm, wv), (wq_hbm, wq)))
    ]
    for load in loads:
        load.start()

    def remote(src, dst, s_sem, r_sem, to):
        return pltpu.make_async_remote_copy(
            src_ref=src, dst_ref=dst, send_sem=s_sem, recv_sem=r_sem,
            device_id={"seq": to}, device_id_type=pl.DeviceIdType.MESH,
        )

    sub = lax.broadcasted_iota(jnp.int32, (LANES, LANES), 0)
    lane = lax.broadcasted_iota(jnp.int32, (LANES, LANES), 1)
    upper = (sub <= lane).astype(f32).astype(bf16)
    counted = dot(ds_ref[...].astype(f32).astype(bf16), upper)
    running = jnp.zeros((1, 1), f32)
    turn[...] = jnp.zeros_like(turn)
    for i in range(tiles):
        turn[i : i + 1, :] = counted[i : i + 1, :] + running
        docs[i : i + 1, :] = counted[i : i + 1, :] + running
        running = running + counted[i : i + 1, LANES - 1 : LANES]
    turn[tiles : 2 * tiles, :] = li_ref[...].astype(f32)
    turned = jnp.transpose(turn[...])
    last_doc = running

    def block_end(r):
        row = (r + 1) * block_tiles - 1
        return docs[row : row + 1, LANES - 1 : LANES]

    dext[0:8, :] = jnp.zeros((8, LANES), f32)
    for i in range(tiles):
        column = jnp.broadcast_to(turned[:, i : i + 1], (LANES, LANES))
        dext[8 + i * LANES : 8 + (i + 1) * LANES, :] = column
        tail[i * LANES : (i + 1) * LANES, :] = (column == block_end(i // block_tiles)).astype(f32).astype(bf16)
    own_open = jnp.broadcast_to((last_doc == 0.0).astype(f32), (8, LANES))
    for part in range(2):
        flag_agg[part] = own_open
        flag_before[part] = jnp.ones((8, LANES), f32)

    loads[0].wait()

    for j in range(width // LANES):
        cols = slice(j * LANES, (j + 1) * LANES)
        rim[:, cols] = tok_ref[rows - EDGE : rows, cols] * tail[rows - EDGE : rows, :]
    pl.semaphore_wait(barrier, len(greeted))
    rim_copy = remote(rim, halo, rim_sem.at[0], rim_sem.at[1], ahead)

    @pl.when(me < count - 1)
    def _():
        rim_copy.start()

    chunk = 64

    def conv_chunk(first):
        ext[pl.ds(8 + first, chunk), :] = tok_ref[pl.ds(first, chunk), :].astype(f32)
        window = pl.ds(first, chunk + 8)
        docs_here = dext[window, :]
        same = [(pltpu.roll(docs_here, t, 0) == docs_here).astype(f32)[8:] for t in range(1, taps)]
        for j in range(width // LANES):
            cols = slice(j * LANES, (j + 1) * LANES)
            values = ext[window, cols]
            total = taps_ref[0:1, cols] * values[8:]
            for t in range(1, taps):
                total = total + taps_ref[t : t + 1, cols] * pltpu.roll(values, t, 0)[8:] * same[t - 1]
            conv[pl.ds(first, chunk), cols] = total.astype(bf16)

    ext[8 : 8 + chunk, :] = tok_ref[0:chunk, :].astype(f32)

    @pl.loop(1, rows // chunk)
    def _(i):
        conv_chunk(pl.multiple_of(i * chunk, chunk))

    @pl.when(me > 0)
    def _():
        rim_copy.wait_recv()

    @pl.when(me == 0)
    def _():
        halo[...] = jnp.zeros_like(halo)

    ext[0:8, :] = halo[...].astype(f32)[EDGE - 8 : EDGE, :]
    conv_chunk(0)

    def project(w, out, i):
        cols = pl.ds(pl.multiple_of(i * 2 * HEAD_DIM, 2 * HEAD_DIM), 2 * HEAD_DIM)
        made = dot(conv[...], w[:, cols]).astype(bf16)
        out[2 * i] = made[:, :HEAD_DIM]
        out[2 * i + 1] = made[:, HEAD_DIM:]

    flag_rows = jnp.concatenate([own_open, own_open], 0).astype(bf16)
    for part in range(2):
        for s in range(2):
            send[0, part, s, part_rows : part_rows + EDGE, :] = flag_rows

    def first(part):
        return remote(send.at[0, part], recv.at[0, part], send_sem.at[0, part], recv_sem.at[0, part], sibling)

    loads[1].wait()
    loads[2].wait()

    @pl.loop(0, HEADS // 2)
    def _(n):
        part, side_of = n // 2, lax.rem(n, 2)
        i = 2 * side_of + part
        project(wk, k, i)
        project(wv, v, i)
        for s in range(2):
            h = 2 * i + s
            sums = []
            for r in range(blocks):
                rows_of = slice(r * block, (r + 1) * block)
                sums.append(dot(k[h, rows_of, :] * tail[rows_of, :], v[h, rows_of, :], ((0,), (0,))))
            for j in range(inner):
                joined = []
                for g in range(0, len(sums), 2):
                    local[h, slots[(g << j, j)]] = sums[g].astype(bf16)
                    linked = (block_end(((g + 2) << j) - 1) == block_end(((g + 1) << j) - 1)).astype(f32)
                    joined.append(sums[g + 1] + linked * sums[g])
                sums = joined
            made = sums[0]
            at = slice(s * HEAD_DIM, (s + 1) * HEAD_DIM)
            state[part, side_of, at, :] = made
            send[0, part, side_of, at, :] = made.astype(bf16)
        for done in range(2):

            @pl.when(n == 2 * done + 1)
            def _():
                first(done).start()

    def step(bit, part):
        return remote(
            send.at[bit, part, core], recv.at[bit, part, core],
            send_sem.at[bit, part], recv_sem.at[bit, part], partner(bit),
        )

    def forward(bit, part):
        return remote(
            recv.at[bit, part, core], recv.at[bit, part, core],
            fwd_send.at[bit, part], fwd_recv.at[bit, part], sibling,
        )

    def note_flags(bit, part):
        other = recv[bit, part, core, part_rows : part_rows + EDGE, :].astype(f32)[0:8]
        right = side(bit).astype(f32)
        before = flag_before[part]
        coef[bit, part] = right * before
        flag_before[part] = before * ((1.0 - right) + right * other)
        return other, right

    def absorb(bit, part):
        other, right = note_flags(bit, part)
        mine = flag_agg[part]
        of_agg = (right + (1.0 - right) * other)[0:1]
        of_other = ((1.0 - right) + right * mine)[0:1]
        source = state[part, core] if bit == 0 else agg[part]
        total = of_agg * source + of_other * recv[bit, part, core, 0:part_rows, :].astype(f32)
        agg[part] = total
        send[bit + 1, part, core, 0:part_rows, :] = total.astype(bf16)
        joined = mine * other
        flag_agg[part] = joined
        send[bit + 1, part, core, part_rows : part_rows + EDGE, :] = jnp.concatenate([joined, joined], 0).astype(bf16)
        step(bit + 1, part).start()

    def arrive(bit, part):
        step(bit, part).wait_recv()
        forward(bit, part).start()
        if bit < bits - 1:
            absorb(bit, part)
        else:
            note_flags(bit, part)

    last = bits - 1
    steps = [(bit, part) for bit in range(1, last) for part in range(2)]
    events = {0: steps[2:3], HEADS - 1: []}
    for n, event in enumerate(steps[3:]):
        after = min(2 + n, HEADS - 1)
        events[after] = events.get(after, []) + [event]
    events[HEADS - 1] = events[HEADS - 1] + [(last, 0)]

    first(0).wait_recv()
    absorb(0, 0)

    loads[3].wait()

    @pl.loop(0, HEADS // 2)
    def _(i):
        project(wq, q, i)

    first(1).wait_recv()
    absorb(0, 1)
    for event in steps[0:1]:
        arrive(*event)

    table = table_ref[...]
    pick = lax.broadcasted_iota(jnp.int32, (LANES, table.shape[1]), 1).astype(f32)
    apart = jnp.bitwise_xor(sub, lane)
    for i in range(tiles):
        chosen = (turned[:, tiles + i : tiles + i + 1] == pick).astype(f32)
        lam[i * LANES : (i + 1) * LANES, :] = dot(chosen, table, ((1,), (1,)), highest)
    for i in range(tiles):
        at = slice(i * LANES, (i + 1) * LANES)
        here = lam[at, :]
        doc = dext[8 + i * LANES : 8 + (i + 1) * LANES, :]

        def spread(level):
            return jnp.broadcast_to(here[:, level : level + 1], (LANES, LANES))

        tile = spread(0)
        for level in range(1, tile_bits + 1):
            tile = jnp.where(apart >= 1 << (level - 1), spread(level), tile)
        wide = {}
        base = i // block_tiles * block_tiles
        for j in range(base, base + block_tiles):
            to = slice((j - base) * LANES, (j - base + 1) * LANES)
            if j > i:
                weight[at, to] = jnp.zeros((LANES, LANES), f32)
            elif j == i:
                weight[at, to] = jnp.where((doc == docs[i : i + 1, :]) & (sub >= lane), tile, 0.0)
            else:
                level = tile_bits + (i ^ j).bit_length()
                if level not in wide:
                    wide[level] = spread(level)
                weight[at, to] = jnp.where(doc == docs[j : j + 1, :], wide[level], 0.0)
        r = i // block_tiles
        for j in range(inner):
            if r >> j & 1:
                before = block_end((r >> j << j) - 1)
                lamloc[j, at, :] = jnp.where(doc == before, spread(block_bits + 1 + j), 0.0)
        for bit in range(bits):
            lamfar[bit, at, :] = jnp.where(doc == 0.0, spread(local_bits + 1 + bit), 0.0)

    for event in steps[1:2]:
        arrive(*event)

    @pl.loop(0, HEADS)
    def _(h):
        for r in range(rows // block):
            at = slice(r * block, (r + 1) * block)
            scores = dot(q[h, at, :], k[h, at, :], ((1,), (1,)))
            weighted = (scores * weight[at, :]).astype(bf16)
            total = dot(weighted, v[h, at, :])
            levels = [j for j in range(inner) if r >> j & 1]
            for a in range(0, len(levels), 2):
                pair = levels[a : a + 2]
                found = [local[h, slots[((r >> j << j) - (1 << j), j)]] for j in pair]
                made = dot(q[h, at, :], jnp.concatenate(found, 1) if len(found) > 1 else found[0])
                for n, j in enumerate(pair):
                    total = total + lamloc[j, at, :] * made[:, n * HEAD_DIM : (n + 1) * HEAD_DIM]
            near[h, at, :] = total
        for after, arriving in events.items():

            @pl.when(h == after)
            def _():
                for event in arriving:
                    arrive(*event)

    def far_state(bit, h):
        part = lax.rem(h, half_heads) // part_heads
        at = pl.ds(pl.multiple_of(lax.rem(h, part_heads) * HEAD_DIM, HEAD_DIM), HEAD_DIM)
        found = recv[bit, part, h // half_heads, at, :].astype(f32)
        return (found * coef[bit, 0][0:1]).astype(bf16)

    for bit in range(1, last):
        for part in range(2):
            forward(bit, part).wait_recv()

    early = list(range(bits - 1))

    @pl.loop(0, HEADS)
    def _(h):
        for r in range(rows // block):
            at = slice(r * block, (r + 1) * block)
            total = near[h, at, :]
            for a in range(0, len(early), 2):
                pair = early[a : a + 2]
                found = [far_state(bit, h) for bit in pair]
                made = dot(q[h, at, :], jnp.concatenate(found, 1) if len(found) > 1 else found[0])
                for n, bit in enumerate(pair):
                    total = total + lamfar[bit, at, :] * made[:, n * HEAD_DIM : (n + 1) * HEAD_DIM]
            near[h, at, :] = total

    arrive(last, 1)

    @pl.loop(0, HEADS)
    def _(n):
        @pl.when(n == half_heads)
        def _():
            for part in range(2):
                forward(last, part).wait_recv()

        h = lax.rem(n + core * half_heads, HEADS)
        cols = pl.ds(pl.multiple_of(h * HEAD_DIM, HEAD_DIM), HEAD_DIM)
        gain = gain_ref[:, cols]
        found = far_state(last, h)
        for r in range(rows // block):
            at = slice(r * block, (r + 1) * block)
            total = near[h, at, :] + lamfar[last, at, :] * dot(q[h, at, :], found)
            scale = lax.rsqrt(jnp.mean(total * total, axis=-1, keepdims=True) + epsilon)
            out_ref[at, cols] = (total * scale * gain).astype(bf16)
        pltpu.make_async_copy(out_ref.at[:, cols], out_hbm.at[:, cols], out_sem.at[h]).start()

    for h in range(HEADS):
        cols = pl.ds(h * HEAD_DIM, HEAD_DIM)
        pltpu.make_async_copy(out_ref.at[:, cols], out_hbm.at[:, cols], out_sem.at[h]).wait()

    @pl.when(me < count - 1)
    def _():
        rim_copy.wait_send()

    for part in range(2):
        first(part).wait_send()
        for bit in range(1, bits):
            step(bit, part).wait_send()
            forward(bit, part).wait_send()


def hand_over(made, out_hbm, held, in_sem, out_sem):
    piece = made.shape[0] // PIECES
    spans = [pl.ds(i * piece, piece) for i in range(PIECES)]
    loads = [pltpu.make_async_copy(made.at[at], held.at[at], in_sem.at[i]) for i, at in enumerate(spans)]
    stores = [pltpu.make_async_copy(held.at[at], out_hbm.at[at], out_sem.at[i]) for i, at in enumerate(spans)]
    for load in loads:
        load.start()
    for load, store in zip(loads, stores):
        load.wait()
        store.start()
    for store in stores:
        store.wait()


def shards(
    tokens, doc_start, level_index, level_table, conv_weight, query_weight, key_weight, value_weight, norm_gain
):
    rows, width = tokens.shape
    count = lax.axis_size("seq")
    bits = count.bit_length() - 1
    part_rows = HEADS // 4 * HEAD_DIM
    heads = (HEADS, rows, HEAD_DIM)
    block = min(2 * LANES, rows)
    inner = (rows // block).bit_length() - 1
    vmem = pl.BlockSpec(memory_space=pltpu.VMEM)
    hbm = pl.BlockSpec(memory_space=pl.ANY)
    dma = pltpu.SemaphoreType.DMA
    made = pl.pallas_call(
        functools.partial(layer, count),
        out_shape=jax.ShapeDtypeStruct((rows, width), bf16),
        in_specs=[vmem] * 5 + [hbm] * 4,
        out_specs=hbm,
        scratch_shapes=[
            pltpu.VMEM((rows, width), bf16),
            pltpu.VMEM((rows, width), bf16),
            pltpu.VMEM((width, width), bf16),
            pltpu.VMEM((width, width), bf16),
            pltpu.VMEM((width, width), bf16),
            pltpu.VMEM((LANES, LANES), f32),
            pltpu.VMEM((rows // LANES, LANES), f32),
            pltpu.VMEM((rows + 8, LANES), f32),
            pltpu.VMEM((rows, LANES), bf16),
            pltpu.VMEM((rows, level_table.shape[1]), f32),
            pltpu.VMEM((bits, rows, LANES), f32),
            pltpu.VMEM((max(inner, 1), rows, LANES), f32),
            pltpu.VMEM((HEADS, max(len(inner_slots(inner)), 1), HEAD_DIM, HEAD_DIM), bf16),
            pltpu.VMEM((rows, block), f32),
            pltpu.VMEM((rows + 8, width), f32),
            pltpu.VMEM((rows, width), bf16),
            pltpu.VMEM(heads, bf16),
            pltpu.VMEM(heads, bf16),
            pltpu.VMEM(heads, bf16),
            pltpu.VMEM(heads, f32),
            pltpu.VMEM((2, 2, part_rows, HEAD_DIM), f32),
            pltpu.VMEM((2, part_rows, HEAD_DIM), f32),
            pltpu.VMEM((2, 8, LANES), f32),
            pltpu.VMEM((2, 8, LANES), f32),
            pltpu.VMEM((bits, 2, 8, LANES), f32),
            pltpu.VMEM((bits, 2, 2, part_rows + EDGE, HEAD_DIM), bf16),
            pltpu.VMEM((bits, 2, 2, part_rows + EDGE, HEAD_DIM), bf16),
            pltpu.VMEM((EDGE, width), bf16),
            pltpu.VMEM((EDGE, width), bf16),
            dma((4,)),
            dma((HEADS,)),
            dma((bits, 2)),
            dma((bits, 2)),
            dma((bits, 2)),
            dma((bits, 2)),
            dma((2,)),
        ],
        compiler_params=pltpu.CompilerParams(
            collective_id=0, has_side_effects=True, vmem_limit_bytes=56 * 1024 * 1024
        ),
    )(
        doc_start.reshape(rows // LANES, LANES),
        level_index.reshape(rows // LANES, LANES),
        level_table.T,
        conv_weight,
        norm_gain.reshape(1, width),
        tokens,
        query_weight,
        key_weight,
        value_weight,
    )
    return pl.pallas_call(
        hand_over,
        out_shape=jax.ShapeDtypeStruct((rows, width), bf16),
        in_specs=[hbm],
        out_specs=hbm,
        scratch_shapes=[pltpu.VMEM((rows, width), bf16), dma((PIECES,)), dma((PIECES,))],
        compiler_params=pltpu.CompilerParams(vmem_limit_bytes=60 * 1024 * 1024),
    )(made)


def solution(mesh):
    split = P(("groups", "seq"))
    rows = P(("groups", "seq"), None)
    in_specs = (rows, split, split, P(), P(), P(), P(), P(), P())
    return jax.shard_map(shards, mesh=mesh, in_specs=in_specs, out_specs=rows, check_vma=False)
```

```python
import functools

import jax
import jax.numpy as jnp
from jax import lax
from jax.experimental import pallas as pl
from jax.experimental.pallas import tpu as pltpu
from jax.sharding import PartitionSpec as P

HEADS = 8
HEAD_DIM = 128
LANES = 128
PIECES = 4
EDGE = 16

highest = lax.Precision.HIGHEST
epsilon = 1e-05
f32 = jnp.float32
bf16 = jnp.bfloat16


def dot(a, b, contract=((1,), (0,)), precision=None):
    return lax.dot_general(a, b, (contract, ((), ())), precision=precision, preferred_element_type=f32)


def inner_slots(inner):
    groups = [(g, j) for j in range(inner) for g in range(0, 1 << inner, 2 << j)]
    return {group: n for n, group in enumerate(groups)}


def layer(
    count,
    ds_ref, li_ref, table_ref, taps_ref, gain_ref, tok_hbm, wq_hbm, wk_hbm, wv_hbm,
    out_hbm,
    tok_ref, out_ref,
    wq, wk, wv, turn, docs, dext, tail, lam, lamfar, lamloc, local, weight, ext, conv, q, k, v, near,
    state, agg, flag_agg, flag_before, coef, send, recv, rim, halo,
    w_sem, out_sem, send_sem, recv_sem, fwd_send, fwd_recv, rim_sem,
):
    rows, width = tok_ref.shape
    tiles = rows // LANES
    taps = taps_ref.shape[0]
    bits = count.bit_length() - 1
    local_bits = rows.bit_length() - 1
    tile_bits = LANES.bit_length() - 1
    block = min(2 * LANES, rows)
    blocks = rows // block
    block_bits = block.bit_length() - 1
    block_tiles = block // LANES
    inner = local_bits - block_bits
    slots = inner_slots(inner)
    half_heads = HEADS // 2
    part_heads = half_heads // 2
    part_rows = part_heads * HEAD_DIM
    me = lax.axis_index("seq")
    core = lax.rem(me, 2)
    sibling = me + 1 - 2 * core

    def side(bit):
        return lax.rem(me // (1 << bit), 2)

    def partner(bit):
        return me + (1 - 2 * side(bit)) * (1 << bit)

    ahead, behind = lax.rem(me + 1, count), lax.rem(me + count - 1, count)
    barrier = pltpu.get_barrier_semaphore()
    greeted = [ahead, behind] + [partner(bit) for bit in range(bits)]
    for other in greeted:
        pl.semaphore_signal(barrier, inc=1, device_id={"seq": other}, device_id_type=pl.DeviceIdType.MESH)

    loads = [
        pltpu.make_async_copy(src, dst, w_sem.at[i])
        for i, (src, dst) in enumerate(((tok_hbm, tok_ref), (wk_hbm, wk), (wv_hbm, wv), (wq_hbm, wq)))
    ]
    for load in loads:
        load.start()

    def remote(src, dst, s_sem, r_sem, to):
        return pltpu.make_async_remote_copy(
            src_ref=src, dst_ref=dst, send_sem=s_sem, recv_sem=r_sem,
            device_id={"seq": to}, device_id_type=pl.DeviceIdType.MESH,
        )

    sub = lax.broadcasted_iota(jnp.int32, (LANES, LANES), 0)
    lane = lax.broadcasted_iota(jnp.int32, (LANES, LANES), 1)
    upper = (sub <= lane).astype(f32).astype(bf16)
    counted = dot(ds_ref[...].astype(f32).astype(bf16), upper)
    running = jnp.zeros((1, 1), f32)
    turn[...] = jnp.zeros_like(turn)
    for i in range(tiles):
        turn[i : i + 1, :] = counted[i : i + 1, :] + running
        docs[i : i + 1, :] = counted[i : i + 1, :] + running
        running = running + counted[i : i + 1, LANES - 1 : LANES]
    turn[tiles : 2 * tiles, :] = li_ref[...].astype(f32)
    turned = jnp.transpose(turn[...])
    last_doc = running

    def block_end(r):
        row = (r + 1) * block_tiles - 1
        return docs[row : row + 1, LANES - 1 : LANES]

    dext[0:8, :] = jnp.zeros((8, LANES), f32)
    for i in range(tiles):
        column = jnp.broadcast_to(turned[:, i : i + 1], (LANES, LANES))
        dext[8 + i * LANES : 8 + (i + 1) * LANES, :] = column
        tail[i * LANES : (i + 1) * LANES, :] = (column == block_end(i // block_tiles)).astype(f32).astype(bf16)
    own_open = jnp.broadcast_to((last_doc == 0.0).astype(f32), (8, LANES))
    for part in range(2):
        flag_agg[part] = own_open
        flag_before[part] = jnp.ones((8, LANES), f32)

    loads[0].wait()

    for j in range(width // LANES):
        cols = slice(j * LANES, (j + 1) * LANES)
        rim[:, cols] = tok_ref[rows - EDGE : rows, cols] * tail[rows - EDGE : rows, :]
    pl.semaphore_wait(barrier, len(greeted))
    rim_copy = remote(rim, halo, rim_sem.at[0], rim_sem.at[1], ahead)

    @pl.when(me < count - 1)
    def _():
        rim_copy.start()

    chunk = 64

    def conv_chunk(first):
        ext[pl.ds(8 + first, chunk), :] = tok_ref[pl.ds(first, chunk), :].astype(f32)
        window = pl.ds(first, chunk + 8)
        docs_here = dext[window, :]
        same = [(pltpu.roll(docs_here, t, 0) == docs_here).astype(f32)[8:] for t in range(1, taps)]
        for j in range(width // LANES):
            cols = slice(j * LANES, (j + 1) * LANES)
            values = ext[window, cols]
            total = taps_ref[0:1, cols] * values[8:]
            for t in range(1, taps):
                total = total + taps_ref[t : t + 1, cols] * pltpu.roll(values, t, 0)[8:] * same[t - 1]
            conv[pl.ds(first, chunk), cols] = total.astype(bf16)

    ext[8 : 8 + chunk, :] = tok_ref[0:chunk, :].astype(f32)

    @pl.loop(1, rows // chunk)
    def _(i):
        conv_chunk(pl.multiple_of(i * chunk, chunk))

    @pl.when(me > 0)
    def _():
        rim_copy.wait_recv()

    @pl.when(me == 0)
    def _():
        halo[...] = jnp.zeros_like(halo)

    ext[0:8, :] = halo[...].astype(f32)[EDGE - 8 : EDGE, :]
    conv_chunk(0)

    def project(w, out, i):
        cols = pl.ds(pl.multiple_of(i * 2 * HEAD_DIM, 2 * HEAD_DIM), 2 * HEAD_DIM)
        made = dot(conv[...], w[:, cols]).astype(bf16)
        out[2 * i] = made[:, :HEAD_DIM]
        out[2 * i + 1] = made[:, HEAD_DIM:]

    flag_rows = jnp.concatenate([own_open, own_open], 0).astype(bf16)
    for part in range(2):
        for s in range(2):
            send[0, part, s, part_rows : part_rows + EDGE, :] = flag_rows

    def first(part):
        return remote(send.at[0, part], recv.at[0, part], send_sem.at[0, part], recv_sem.at[0, part], sibling)

    loads[1].wait()
    loads[2].wait()

    @pl.loop(0, HEADS // 2)
    def _(n):
        part, side_of = n // 2, lax.rem(n, 2)
        i = 2 * side_of + part
        project(wk, k, i)
        project(wv, v, i)
        for s in range(2):
            h = 2 * i + s
            sums = []
            for r in range(blocks):
                rows_of = slice(r * block, (r + 1) * block)
                sums.append(dot(k[h, rows_of, :] * tail[rows_of, :], v[h, rows_of, :], ((0,), (0,))))
            for j in range(inner):
                joined = []
                for g in range(0, len(sums), 2):
                    local[h, slots[(g << j, j)]] = sums[g].astype(bf16)
                    linked = (block_end(((g + 2) << j) - 1) == block_end(((g + 1) << j) - 1)).astype(f32)
                    joined.append(sums[g + 1] + linked * sums[g])
                sums = joined
            made = sums[0]
            at = slice(s * HEAD_DIM, (s + 1) * HEAD_DIM)
            state[part, side_of, at, :] = made
            send[0, part, side_of, at, :] = made.astype(bf16)
        for done in range(2):

            @pl.when(n == 2 * done + 1)
            def _():
                first(done).start()

    def step(bit, part):
        return remote(
            send.at[bit, part, core], recv.at[bit, part, core],
            send_sem.at[bit, part], recv_sem.at[bit, part], partner(bit),
        )

    def forward(bit, part):
        return remote(
            recv.at[bit, part, core], recv.at[bit, part, core],
            fwd_send.at[bit, part], fwd_recv.at[bit, part], sibling,
        )

    def note_flags(bit, part):
        other = recv[bit, part, core, part_rows : part_rows + EDGE, :].astype(f32)[0:8]
        right = side(bit).astype(f32)
        before = flag_before[part]
        coef[bit, part] = right * before
        flag_before[part] = before * ((1.0 - right) + right * other)
        return other, right

    def absorb(bit, part):
        other, right = note_flags(bit, part)
        mine = flag_agg[part]
        of_agg = (right + (1.0 - right) * other)[0:1]
        of_other = ((1.0 - right) + right * mine)[0:1]
        source = state[part, core] if bit == 0 else agg[part]
        total = of_agg * source + of_other * recv[bit, part, core, 0:part_rows, :].astype(f32)
        agg[part] = total
        send[bit + 1, part, core, 0:part_rows, :] = total.astype(bf16)
        joined = mine * other
        flag_agg[part] = joined
        send[bit + 1, part, core, part_rows : part_rows + EDGE, :] = jnp.concatenate([joined, joined], 0).astype(bf16)
        step(bit + 1, part).start()

    def arrive(bit, part):
        step(bit, part).wait_recv()
        forward(bit, part).start()
        if bit < bits - 1:
            absorb(bit, part)
        else:
            note_flags(bit, part)

    last = bits - 1
    steps = [(bit, part) for bit in range(1, last) for part in range(2)]
    events = {0: steps[2:3], HEADS - 1: []}
    for n, event in enumerate(steps[3:]):
        after = min(2 + n, HEADS - 1)
        events[after] = events.get(after, []) + [event]
    events[HEADS - 1] = events[HEADS - 1] + [(last, 0)]

    first(0).wait_recv()
    absorb(0, 0)

    loads[3].wait()

    @pl.loop(0, HEADS // 2)
    def _(i):
        project(wq, q, i)

        @pl.when(i == HEADS // 4 - 1)
        def _():
            first(1).wait_recv()
            absorb(0, 1)

    for event in steps[0:1]:
        arrive(*event)

    table = table_ref[...]
    pick = lax.broadcasted_iota(jnp.int32, (LANES, table.shape[1]), 1).astype(f32)
    apart = jnp.bitwise_xor(sub, lane)
    for i in range(tiles):
        chosen = (turned[:, tiles + i : tiles + i + 1] == pick).astype(f32)
        lam[i * LANES : (i + 1) * LANES, :] = dot(chosen, table, ((1,), (1,)), highest)
    for i in range(tiles):
        at = slice(i * LANES, (i + 1) * LANES)
        here = lam[at, :]
        doc = dext[8 + i * LANES : 8 + (i + 1) * LANES, :]

        def spread(level):
            return jnp.broadcast_to(here[:, level : level + 1], (LANES, LANES))

        tile = spread(0)
        for level in range(1, tile_bits + 1):
            tile = jnp.where(apart >= 1 << (level - 1), spread(level), tile)
        wide = {}
        base = i // block_tiles * block_tiles
        for j in range(base, base + block_tiles):
            to = slice((j - base) * LANES, (j - base + 1) * LANES)
            if j > i:
                weight[at, to] = jnp.zeros((LANES, LANES), f32)
            elif j == i:
                weight[at, to] = jnp.where((doc == docs[i : i + 1, :]) & (sub >= lane), tile, 0.0)
            else:
                level = tile_bits + (i ^ j).bit_length()
                if level not in wide:
                    wide[level] = spread(level)
                weight[at, to] = jnp.where(doc == docs[j : j + 1, :], wide[level], 0.0)
        r = i // block_tiles
        for j in range(inner):
            if r >> j & 1:
                before = block_end((r >> j << j) - 1)
                lamloc[j, at, :] = jnp.where(doc == before, spread(block_bits + 1 + j), 0.0)
        for bit in range(bits):
            lamfar[bit, at, :] = jnp.where(doc == 0.0, spread(local_bits + 1 + bit), 0.0)

    for event in steps[1:2]:
        arrive(*event)

    @pl.loop(0, HEADS)
    def _(h):
        for r in range(rows // block):
            at = slice(r * block, (r + 1) * block)
            scores = dot(q[h, at, :], k[h, at, :], ((1,), (1,)))
            weighted = (scores * weight[at, :]).astype(bf16)
            total = dot(weighted, v[h, at, :])
            levels = [j for j in range(inner) if r >> j & 1]
            for a in range(0, len(levels), 2):
                pair = levels[a : a + 2]
                found = [local[h, slots[((r >> j << j) - (1 << j), j)]] for j in pair]
                made = dot(q[h, at, :], jnp.concatenate(found, 1) if len(found) > 1 else found[0])
                for n, j in enumerate(pair):
                    total = total + lamloc[j, at, :] * made[:, n * HEAD_DIM : (n + 1) * HEAD_DIM]
            near[h, at, :] = total
        for after, arriving in events.items():

            @pl.when(h == after)
            def _():
                for event in arriving:
                    arrive(*event)

    def far_state(bit, h):
        part = lax.rem(h, half_heads) // part_heads
        at = pl.ds(pl.multiple_of(lax.rem(h, part_heads) * HEAD_DIM, HEAD_DIM), HEAD_DIM)
        found = recv[bit, part, h // half_heads, at, :].astype(f32)
        return (found * coef[bit, 0][0:1]).astype(bf16)

    for bit in range(1, last):
        for part in range(2):
            forward(bit, part).wait_recv()

    early = list(range(bits - 1))

    @pl.loop(0, HEADS)
    def _(h):
        for r in range(rows // block):
            at = slice(r * block, (r + 1) * block)
            total = near[h, at, :]
            for a in range(0, len(early), 2):
                pair = early[a : a + 2]
                found = [far_state(bit, h) for bit in pair]
                made = dot(q[h, at, :], jnp.concatenate(found, 1) if len(found) > 1 else found[0])
                for n, bit in enumerate(pair):
                    total = total + lamfar[bit, at, :] * made[:, n * HEAD_DIM : (n + 1) * HEAD_DIM]
            near[h, at, :] = total

    @pl.loop(0, HEADS)
    def _(n):
        @pl.when(n == part_heads)
        def _():
            forward(last, 0).wait_recv()

        @pl.when(n == half_heads)
        def _():
            arrive(last, 1)

        @pl.when(n == half_heads + part_heads)
        def _():
            forward(last, 1).wait_recv()

        of_half = lax.rem(lax.rem(n // part_heads, 2) + core, 2)
        h = of_half * half_heads + n // half_heads * part_heads + lax.rem(n, part_heads)
        cols = pl.ds(pl.multiple_of(h * HEAD_DIM, HEAD_DIM), HEAD_DIM)
        gain = gain_ref[:, cols]
        found = far_state(last, h)
        for r in range(rows // block):
            at = slice(r * block, (r + 1) * block)
            total = near[h, at, :] + lamfar[last, at, :] * dot(q[h, at, :], found)
            scale = lax.rsqrt(jnp.mean(total * total, axis=-1, keepdims=True) + epsilon)
            out_ref[at, cols] = (total * scale * gain).astype(bf16)
        pltpu.make_async_copy(out_ref.at[:, cols], out_hbm.at[:, cols], out_sem.at[h]).start()

    for h in range(HEADS):
        cols = pl.ds(h * HEAD_DIM, HEAD_DIM)
        pltpu.make_async_copy(out_ref.at[:, cols], out_hbm.at[:, cols], out_sem.at[h]).wait()

    @pl.when(me < count - 1)
    def _():
        rim_copy.wait_send()

    for part in range(2):
        first(part).wait_send()
        for bit in range(1, bits):
            step(bit, part).wait_send()
            forward(bit, part).wait_send()


def hand_over(made, out_hbm, held, in_sem, out_sem):
    piece = made.shape[0] // PIECES
    spans = [pl.ds(i * piece, piece) for i in range(PIECES)]
    loads = [pltpu.make_async_copy(made.at[at], held.at[at], in_sem.at[i]) for i, at in enumerate(spans)]
    stores = [pltpu.make_async_copy(held.at[at], out_hbm.at[at], out_sem.at[i]) for i, at in enumerate(spans)]
    for load in loads:
        load.start()
    for load, store in zip(loads, stores):
        load.wait()
        store.start()
    for store in stores:
        store.wait()


def shards(
    tokens, doc_start, level_index, level_table, conv_weight, query_weight, key_weight, value_weight, norm_gain
):
    rows, width = tokens.shape
    count = lax.axis_size("seq")
    bits = count.bit_length() - 1
    part_rows = HEADS // 4 * HEAD_DIM
    heads = (HEADS, rows, HEAD_DIM)
    block = min(2 * LANES, rows)
    inner = (rows // block).bit_length() - 1
    vmem = pl.BlockSpec(memory_space=pltpu.VMEM)
    hbm = pl.BlockSpec(memory_space=pl.ANY)
    dma = pltpu.SemaphoreType.DMA
    made = pl.pallas_call(
        functools.partial(layer, count),
        out_shape=jax.ShapeDtypeStruct((rows, width), bf16),
        in_specs=[vmem] * 5 + [hbm] * 4,
        out_specs=hbm,
        scratch_shapes=[
            pltpu.VMEM((rows, width), bf16),
            pltpu.VMEM((rows, width), bf16),
            pltpu.VMEM((width, width), bf16),
            pltpu.VMEM((width, width), bf16),
            pltpu.VMEM((width, width), bf16),
            pltpu.VMEM((LANES, LANES), f32),
            pltpu.VMEM((rows // LANES, LANES), f32),
            pltpu.VMEM((rows + 8, LANES), f32),
            pltpu.VMEM((rows, LANES), bf16),
            pltpu.VMEM((rows, level_table.shape[1]), f32),
            pltpu.VMEM((bits, rows, LANES), f32),
            pltpu.VMEM((max(inner, 1), rows, LANES), f32),
            pltpu.VMEM((HEADS, max(len(inner_slots(inner)), 1), HEAD_DIM, HEAD_DIM), bf16),
            pltpu.VMEM((rows, block), f32),
            pltpu.VMEM((rows + 8, width), f32),
            pltpu.VMEM((rows, width), bf16),
            pltpu.VMEM(heads, bf16),
            pltpu.VMEM(heads, bf16),
            pltpu.VMEM(heads, bf16),
            pltpu.VMEM(heads, f32),
            pltpu.VMEM((2, 2, part_rows, HEAD_DIM), f32),
            pltpu.VMEM((2, part_rows, HEAD_DIM), f32),
            pltpu.VMEM((2, 8, LANES), f32),
            pltpu.VMEM((2, 8, LANES), f32),
            pltpu.VMEM((bits, 2, 8, LANES), f32),
            pltpu.VMEM((bits, 2, 2, part_rows + EDGE, HEAD_DIM), bf16),
            pltpu.VMEM((bits, 2, 2, part_rows + EDGE, HEAD_DIM), bf16),
            pltpu.VMEM((EDGE, width), bf16),
            pltpu.VMEM((EDGE, width), bf16),
            dma((4,)),
            dma((HEADS,)),
            dma((bits, 2)),
            dma((bits, 2)),
            dma((bits, 2)),
            dma((bits, 2)),
            dma((2,)),
        ],
        compiler_params=pltpu.CompilerParams(
            collective_id=0, has_side_effects=True, vmem_limit_bytes=56 * 1024 * 1024
        ),
    )(
        doc_start.reshape(rows // LANES, LANES),
        level_index.reshape(rows // LANES, LANES),
        level_table.T,
        conv_weight,
        norm_gain.reshape(1, width),
        tokens,
        query_weight,
        key_weight,
        value_weight,
    )
    return pl.pallas_call(
        hand_over,
        out_shape=jax.ShapeDtypeStruct((rows, width), bf16),
        in_specs=[hbm],
        out_specs=hbm,
        scratch_shapes=[pltpu.VMEM((rows, width), bf16), dma((PIECES,)), dma((PIECES,))],
        compiler_params=pltpu.CompilerParams(vmem_limit_bytes=60 * 1024 * 1024),
    )(made)


def solution(mesh):
    split = P(("groups", "seq"))
    rows = P(("groups", "seq"), None)
    in_specs = (rows, split, split, P(), P(), P(), P(), P(), P())
    return jax.shard_map(shards, mesh=mesh, in_specs=in_specs, out_specs=rows, check_vma=False)
```

```python
import functools

import jax
import jax.numpy as jnp
from jax import lax
from jax.experimental import pallas as pl
from jax.experimental.pallas import tpu as pltpu
from jax.sharding import PartitionSpec as P

HEADS = 8
HEAD_DIM = 128
LANES = 128
PIECES = 4
EDGE = 16

highest = lax.Precision.HIGHEST
epsilon = 1e-05
f32 = jnp.float32
bf16 = jnp.bfloat16


def dot(a, b, contract=((1,), (0,)), precision=None):
    return lax.dot_general(a, b, (contract, ((), ())), precision=precision, preferred_element_type=f32)


def inner_slots(inner):
    groups = [(g, j) for j in range(inner) for g in range(0, 1 << inner, 2 << j)]
    return {group: n for n, group in enumerate(groups)}


def layer(
    count,
    ds_ref, li_ref, table_ref, taps_ref, gain_ref, tok_hbm, wq_hbm, wk_hbm, wv_hbm,
    out_hbm,
    tok_ref, out_ref,
    wq, wk, wv, turn, docs, dext, tail, lam, lamfar, lamloc, local, weight, ext, conv, q, k, v, near,
    state, agg, flag_agg, flag_before, coef, send, recv, rim, halo,
    w_sem, out_sem, send_sem, recv_sem, fwd_send, fwd_recv, rim_sem,
):
    rows, width = tok_ref.shape
    tiles = rows // LANES
    taps = taps_ref.shape[0]
    bits = count.bit_length() - 1
    local_bits = rows.bit_length() - 1
    tile_bits = LANES.bit_length() - 1
    block = min(2 * LANES, rows)
    blocks = rows // block
    block_bits = block.bit_length() - 1
    block_tiles = block // LANES
    inner = local_bits - block_bits
    slots = inner_slots(inner)
    half_heads = HEADS // 2
    part_heads = half_heads // 2
    part_rows = part_heads * HEAD_DIM
    me = lax.axis_index("seq")
    core = lax.rem(me, 2)
    sibling = me + 1 - 2 * core

    def side(bit):
        return lax.rem(me // (1 << bit), 2)

    def partner(bit):
        return me + (1 - 2 * side(bit)) * (1 << bit)

    ahead, behind = lax.rem(me + 1, count), lax.rem(me + count - 1, count)
    barrier = pltpu.get_barrier_semaphore()
    greeted = [ahead, behind] + [partner(bit) for bit in range(bits)]
    for other in greeted:
        pl.semaphore_signal(barrier, inc=1, device_id={"seq": other}, device_id_type=pl.DeviceIdType.MESH)

    loads = [
        pltpu.make_async_copy(src, dst, w_sem.at[i])
        for i, (src, dst) in enumerate(((tok_hbm, tok_ref), (wk_hbm, wk), (wv_hbm, wv), (wq_hbm, wq)))
    ]
    loads[0].start()

    def remote(src, dst, s_sem, r_sem, to):
        return pltpu.make_async_remote_copy(
            src_ref=src, dst_ref=dst, send_sem=s_sem, recv_sem=r_sem,
            device_id={"seq": to}, device_id_type=pl.DeviceIdType.MESH,
        )

    sub = lax.broadcasted_iota(jnp.int32, (LANES, LANES), 0)
    lane = lax.broadcasted_iota(jnp.int32, (LANES, LANES), 1)
    upper = (sub <= lane).astype(f32).astype(bf16)
    counted = dot(ds_ref[...].astype(f32).astype(bf16), upper)
    running = jnp.zeros((1, 1), f32)
    turn[...] = jnp.zeros_like(turn)
    for i in range(tiles):
        turn[i : i + 1, :] = counted[i : i + 1, :] + running
        docs[i : i + 1, :] = counted[i : i + 1, :] + running
        running = running + counted[i : i + 1, LANES - 1 : LANES]
    turn[tiles : 2 * tiles, :] = li_ref[...].astype(f32)
    turned = jnp.transpose(turn[...])
    last_doc = running

    def block_end(r):
        row = (r + 1) * block_tiles - 1
        return docs[row : row + 1, LANES - 1 : LANES]

    dext[0:8, :] = jnp.zeros((8, LANES), f32)
    for i in range(tiles):
        column = jnp.broadcast_to(turned[:, i : i + 1], (LANES, LANES))
        dext[8 + i * LANES : 8 + (i + 1) * LANES, :] = column
        tail[i * LANES : (i + 1) * LANES, :] = (column == block_end(i // block_tiles)).astype(f32).astype(bf16)
    own_open = jnp.broadcast_to((last_doc == 0.0).astype(f32), (8, LANES))
    for part in range(2):
        flag_agg[part] = own_open
        flag_before[part] = jnp.ones((8, LANES), f32)

    loads[0].wait()
    for load in loads[1:]:
        load.start()

    for j in range(width // LANES):
        cols = slice(j * LANES, (j + 1) * LANES)
        rim[:, cols] = tok_ref[rows - EDGE : rows, cols] * tail[rows - EDGE : rows, :]
    pl.semaphore_wait(barrier, len(greeted))
    rim_copy = remote(rim, halo, rim_sem.at[0], rim_sem.at[1], ahead)

    @pl.when(me < count - 1)
    def _():
        rim_copy.start()

    chunk = 64

    def conv_chunk(first):
        ext[pl.ds(8 + first, chunk), :] = tok_ref[pl.ds(first, chunk), :].astype(f32)
        window = pl.ds(first, chunk + 8)
        docs_here = dext[window, :]
        same = [(pltpu.roll(docs_here, t, 0) == docs_here).astype(f32)[8:] for t in range(1, taps)]
        for j in range(width // LANES):
            cols = slice(j * LANES, (j + 1) * LANES)
            values = ext[window, cols]
            total = taps_ref[0:1, cols] * values[8:]
            for t in range(1, taps):
                total = total + taps_ref[t : t + 1, cols] * pltpu.roll(values, t, 0)[8:] * same[t - 1]
            conv[pl.ds(first, chunk), cols] = total.astype(bf16)

    ext[8 : 8 + chunk, :] = tok_ref[0:chunk, :].astype(f32)

    @pl.loop(1, rows // chunk)
    def _(i):
        conv_chunk(pl.multiple_of(i * chunk, chunk))

    @pl.when(me > 0)
    def _():
        rim_copy.wait_recv()

    @pl.when(me == 0)
    def _():
        halo[...] = jnp.zeros_like(halo)

    ext[0:8, :] = halo[...].astype(f32)[EDGE - 8 : EDGE, :]
    conv_chunk(0)

    def project(w, out, i):
        cols = pl.ds(pl.multiple_of(i * 2 * HEAD_DIM, 2 * HEAD_DIM), 2 * HEAD_DIM)
        made = dot(conv[...], w[:, cols]).astype(bf16)
        out[2 * i] = made[:, :HEAD_DIM]
        out[2 * i + 1] = made[:, HEAD_DIM:]

    flag_rows = jnp.concatenate([own_open, own_open], 0).astype(bf16)
    for part in range(2):
        for s in range(2):
            send[0, part, s, part_rows : part_rows + EDGE, :] = flag_rows

    def first(part):
        return remote(send.at[0, part], recv.at[0, part], send_sem.at[0, part], recv_sem.at[0, part], sibling)

    loads[1].wait()
    loads[2].wait()

    @pl.loop(0, HEADS // 2)
    def _(n):
        part, side_of = n // 2, lax.rem(n, 2)
        i = 2 * side_of + part
        project(wk, k, i)
        project(wv, v, i)
        for s in range(2):
            h = 2 * i + s
            sums = []
            for r in range(blocks):
                rows_of = slice(r * block, (r + 1) * block)
                sums.append(dot(k[h, rows_of, :] * tail[rows_of, :], v[h, rows_of, :], ((0,), (0,))))
            for j in range(inner):
                joined = []
                for g in range(0, len(sums), 2):
                    local[h, slots[(g << j, j)]] = sums[g].astype(bf16)
                    linked = (block_end(((g + 2) << j) - 1) == block_end(((g + 1) << j) - 1)).astype(f32)
                    joined.append(sums[g + 1] + linked * sums[g])
                sums = joined
            made = sums[0]
            at = slice(s * HEAD_DIM, (s + 1) * HEAD_DIM)
            state[part, side_of, at, :] = made
            send[0, part, side_of, at, :] = made.astype(bf16)
        for done in range(2):

            @pl.when(n == 2 * done + 1)
            def _():
                first(done).start()

    def step(bit, part):
        return remote(
            send.at[bit, part, core], recv.at[bit, part, core],
            send_sem.at[bit, part], recv_sem.at[bit, part], partner(bit),
        )

    def forward(bit, part):
        return remote(
            recv.at[bit, part, core], recv.at[bit, part, core],
            fwd_send.at[bit, part], fwd_recv.at[bit, part], sibling,
        )

    def note_flags(bit, part):
        other = recv[bit, part, core, part_rows : part_rows + EDGE, :].astype(f32)[0:8]
        right = side(bit).astype(f32)
        before = flag_before[part]
        coef[bit, part] = right * before
        flag_before[part] = before * ((1.0 - right) + right * other)
        return other, right

    def absorb(bit, part):
        other, right = note_flags(bit, part)
        mine = flag_agg[part]
        of_agg = (right + (1.0 - right) * other)[0:1]
        of_other = ((1.0 - right) + right * mine)[0:1]
        source = state[part, core] if bit == 0 else agg[part]
        total = of_agg * source + of_other * recv[bit, part, core, 0:part_rows, :].astype(f32)
        agg[part] = total
        send[bit + 1, part, core, 0:part_rows, :] = total.astype(bf16)
        joined = mine * other
        flag_agg[part] = joined
        send[bit + 1, part, core, part_rows : part_rows + EDGE, :] = jnp.concatenate([joined, joined], 0).astype(bf16)
        step(bit + 1, part).start()

    def arrive(bit, part):
        step(bit, part).wait_recv()
        forward(bit, part).start()
        if bit < bits - 1:
            absorb(bit, part)
        else:
            note_flags(bit, part)

    last = bits - 1
    steps = [(bit, part) for bit in range(1, last) for part in range(2)]
    events = {0: steps[2:3], HEADS - 1: []}
    for n, event in enumerate(steps[3:]):
        after = min(2 + n, HEADS - 1)
        events[after] = events.get(after, []) + [event]
    events[HEADS - 1] = events[HEADS - 1] + [(last, 0)]

    first(0).wait_recv()
    absorb(0, 0)

    table = table_ref[...]
    pick = lax.broadcasted_iota(jnp.int32, (LANES, table.shape[1]), 1).astype(f32)
    apart = jnp.bitwise_xor(sub, lane)
    for i in range(tiles):
        chosen = (turned[:, tiles + i : tiles + i + 1] == pick).astype(f32)
        lam[i * LANES : (i + 1) * LANES, :] = dot(chosen, table, ((1,), (1,)), highest)
    def build(i):
        at = slice(i * LANES, (i + 1) * LANES)
        here = lam[at, :]
        doc = dext[8 + i * LANES : 8 + (i + 1) * LANES, :]

        def spread(level):
            return jnp.broadcast_to(here[:, level : level + 1], (LANES, LANES))

        tile = spread(0)
        for level in range(1, tile_bits + 1):
            tile = jnp.where(apart >= 1 << (level - 1), spread(level), tile)
        wide = {}
        base = i // block_tiles * block_tiles
        for j in range(base, base + block_tiles):
            to = slice((j - base) * LANES, (j - base + 1) * LANES)
            if j > i:
                weight[at, to] = jnp.zeros((LANES, LANES), f32)
            elif j == i:
                weight[at, to] = jnp.where((doc == docs[i : i + 1, :]) & (sub >= lane), tile, 0.0)
            else:
                level = tile_bits + (i ^ j).bit_length()
                if level not in wide:
                    wide[level] = spread(level)
                weight[at, to] = jnp.where(doc == docs[j : j + 1, :], wide[level], 0.0)
        r = i // block_tiles
        for j in range(inner):
            if r >> j & 1:
                before = block_end((r >> j << j) - 1)
                lamloc[j, at, :] = jnp.where(doc == before, spread(block_bits + 1 + j), 0.0)
        for bit in range(bits):
            lamfar[bit, at, :] = jnp.where(doc == 0.0, spread(local_bits + 1 + bit), 0.0)

    loads[3].wait()
    pairs = HEADS // 2
    for n in range(pairs):
        project(wq, q, n)
        for i in range(n * tiles // pairs, (n + 1) * tiles // pairs):
            build(i)
        if n == pairs // 2 - 1:
            first(1).wait_recv()
            absorb(0, 1)
        elif n == pairs - 2:
            for event in steps[0:1]:
                arrive(*event)
    for event in steps[1:2]:
        arrive(*event)

    @pl.loop(0, HEADS)
    def _(h):
        for r in range(rows // block):
            at = slice(r * block, (r + 1) * block)
            scores = dot(q[h, at, :], k[h, at, :], ((1,), (1,)))
            weighted = (scores * weight[at, :]).astype(bf16)
            total = dot(weighted, v[h, at, :])
            levels = [j for j in range(inner) if r >> j & 1]
            for a in range(0, len(levels), 2):
                pair = levels[a : a + 2]
                found = [local[h, slots[((r >> j << j) - (1 << j), j)]] for j in pair]
                made = dot(q[h, at, :], jnp.concatenate(found, 1) if len(found) > 1 else found[0])
                for n, j in enumerate(pair):
                    total = total + lamloc[j, at, :] * made[:, n * HEAD_DIM : (n + 1) * HEAD_DIM]
            near[h, at, :] = total
        for after, arriving in events.items():

            @pl.when(h == after)
            def _():
                for event in arriving:
                    arrive(*event)

    def far_state(bit, h):
        part = lax.rem(h, half_heads) // part_heads
        at = pl.ds(pl.multiple_of(lax.rem(h, part_heads) * HEAD_DIM, HEAD_DIM), HEAD_DIM)
        found = recv[bit, part, h // half_heads, at, :].astype(f32)
        return (found * coef[bit, 0][0:1]).astype(bf16)

    for bit in range(1, last):
        for part in range(2):
            forward(bit, part).wait_recv()

    early = list(range(bits - 1))

    @pl.loop(0, HEADS)
    def _(h):
        for r in range(rows // block):
            at = slice(r * block, (r + 1) * block)
            total = near[h, at, :]
            for a in range(0, len(early), 2):
                pair = early[a : a + 2]
                found = [far_state(bit, h) for bit in pair]
                made = dot(q[h, at, :], jnp.concatenate(found, 1) if len(found) > 1 else found[0])
                for n, bit in enumerate(pair):
                    total = total + lamfar[bit, at, :] * made[:, n * HEAD_DIM : (n + 1) * HEAD_DIM]
            near[h, at, :] = total

    @pl.loop(0, HEADS)
    def _(n):
        @pl.when(n == part_heads)
        def _():
            forward(last, 0).wait_recv()

        @pl.when(n == half_heads)
        def _():
            arrive(last, 1)

        @pl.when(n == half_heads + part_heads)
        def _():
            forward(last, 1).wait_recv()

        of_half = lax.rem(lax.rem(n // part_heads, 2) + core, 2)
        h = of_half * half_heads + n // half_heads * part_heads + lax.rem(n, part_heads)
        cols = pl.ds(pl.multiple_of(h * HEAD_DIM, HEAD_DIM), HEAD_DIM)
        gain = gain_ref[:, cols]
        found = far_state(last, h)
        for r in range(rows // block):
            at = slice(r * block, (r + 1) * block)
            total = near[h, at, :] + lamfar[last, at, :] * dot(q[h, at, :], found)
            scale = lax.rsqrt(jnp.mean(total * total, axis=-1, keepdims=True) + epsilon)
            out_ref[at, cols] = (total * scale * gain).astype(bf16)
        pltpu.make_async_copy(out_ref.at[:, cols], out_hbm.at[:, cols], out_sem.at[h]).start()

    for h in range(HEADS):
        cols = pl.ds(h * HEAD_DIM, HEAD_DIM)
        pltpu.make_async_copy(out_ref.at[:, cols], out_hbm.at[:, cols], out_sem.at[h]).wait()

    @pl.when(me < count - 1)
    def _():
        rim_copy.wait_send()

    for part in range(2):
        first(part).wait_send()
        for bit in range(1, bits):
            step(bit, part).wait_send()
            forward(bit, part).wait_send()


def hand_over(made, out_hbm, held, in_sem, out_sem):
    piece = made.shape[0] // PIECES
    spans = [pl.ds(i * piece, piece) for i in range(PIECES)]
    loads = [pltpu.make_async_copy(made.at[at], held.at[at], in_sem.at[i]) for i, at in enumerate(spans)]
    stores = [pltpu.make_async_copy(held.at[at], out_hbm.at[at], out_sem.at[i]) for i, at in enumerate(spans)]
    for load in loads:
        load.start()
    for load, store in zip(loads, stores):
        load.wait()
        store.start()
    for store in stores:
        store.wait()


def shards(
    tokens, doc_start, level_index, level_table, conv_weight, query_weight, key_weight, value_weight, norm_gain
):
    rows, width = tokens.shape
    count = lax.axis_size("seq")
    bits = count.bit_length() - 1
    part_rows = HEADS // 4 * HEAD_DIM
    heads = (HEADS, rows, HEAD_DIM)
    block = min(2 * LANES, rows)
    inner = (rows // block).bit_length() - 1
    vmem = pl.BlockSpec(memory_space=pltpu.VMEM)
    hbm = pl.BlockSpec(memory_space=pl.ANY)
    dma = pltpu.SemaphoreType.DMA
    made = pl.pallas_call(
        functools.partial(layer, count),
        out_shape=jax.ShapeDtypeStruct((rows, width), bf16),
        in_specs=[vmem] * 5 + [hbm] * 4,
        out_specs=hbm,
        scratch_shapes=[
            pltpu.VMEM((rows, width), bf16),
            pltpu.VMEM((rows, width), bf16),
            pltpu.VMEM((width, width), bf16),
            pltpu.VMEM((width, width), bf16),
            pltpu.VMEM((width, width), bf16),
            pltpu.VMEM((LANES, LANES), f32),
            pltpu.VMEM((rows // LANES, LANES), f32),
            pltpu.VMEM((rows + 8, LANES), f32),
            pltpu.VMEM((rows, LANES), bf16),
            pltpu.VMEM((rows, level_table.shape[1]), f32),
            pltpu.VMEM((bits, rows, LANES), f32),
            pltpu.VMEM((max(inner, 1), rows, LANES), f32),
            pltpu.VMEM((HEADS, max(len(inner_slots(inner)), 1), HEAD_DIM, HEAD_DIM), bf16),
            pltpu.VMEM((rows, block), f32),
            pltpu.VMEM((rows + 8, width), f32),
            pltpu.VMEM((rows, width), bf16),
            pltpu.VMEM(heads, bf16),
            pltpu.VMEM(heads, bf16),
            pltpu.VMEM(heads, bf16),
            pltpu.VMEM(heads, f32),
            pltpu.VMEM((2, 2, part_rows, HEAD_DIM), f32),
            pltpu.VMEM((2, part_rows, HEAD_DIM), f32),
            pltpu.VMEM((2, 8, LANES), f32),
            pltpu.VMEM((2, 8, LANES), f32),
            pltpu.VMEM((bits, 2, 8, LANES), f32),
            pltpu.VMEM((bits, 2, 2, part_rows + EDGE, HEAD_DIM), bf16),
            pltpu.VMEM((bits, 2, 2, part_rows + EDGE, HEAD_DIM), bf16),
            pltpu.VMEM((EDGE, width), bf16),
            pltpu.VMEM((EDGE, width), bf16),
            dma((4,)),
            dma((HEADS,)),
            dma((bits, 2)),
            dma((bits, 2)),
            dma((bits, 2)),
            dma((bits, 2)),
            dma((2,)),
        ],
        compiler_params=pltpu.CompilerParams(
            collective_id=0, has_side_effects=True, vmem_limit_bytes=56 * 1024 * 1024
        ),
    )(
        doc_start.reshape(rows // LANES, LANES),
        level_index.reshape(rows // LANES, LANES),
        level_table.T,
        conv_weight,
        norm_gain.reshape(1, width),
        tokens,
        query_weight,
        key_weight,
        value_weight,
    )
    return pl.pallas_call(
        hand_over,
        out_shape=jax.ShapeDtypeStruct((rows, width), bf16),
        in_specs=[hbm],
        out_specs=hbm,
        scratch_shapes=[pltpu.VMEM((rows, width), bf16), dma((PIECES,)), dma((PIECES,))],
        compiler_params=pltpu.CompilerParams(vmem_limit_bytes=60 * 1024 * 1024),
    )(made)


def solution(mesh):
    split = P(("groups", "seq"))
    rows = P(("groups", "seq"), None)
    in_specs = (rows, split, split, P(), P(), P(), P(), P(), P())
    return jax.shard_map(shards, mesh=mesh, in_specs=in_specs, out_specs=rows, check_vma=False)
```
